32 devices in a mesh: seq: 8 (over z, x), mp: 4 (over y, core).
Axes of the slice: x: 2, y: 2, z: 4, core: 2. Of those that a mesh axis runs over, the one named last changes fastest.
Arguments:
- win_query: bfloat16 [4096, 4096], P('seq', 'mp'), may hold values from -8 to 8
- win_key: bfloat16 [4096, 4096], P('seq', 'mp'), may hold values from -8 to 8
- win_value: bfloat16 [4096, 4096], P('seq', 'mp'), may hold values from -6 to 6
- win_dout: bfloat16 [4096, 4096], P('seq', 'mp'), may hold values from -16 to 16
- cross_query: bfloat16 [4096, 4096], P('seq', 'mp'), may hold values from -8 to 8
- cross_dout: bfloat16 [4096, 4096], P('seq', 'mp'), may hold values from -16 to 16
- patch_key: bfloat16 [1024, 4096], P('seq', 'mp'), may hold values from -8 to 8
- patch_value: bfloat16 [1024, 4096], P('seq', 'mp'), may hold values from -6 to 6
- patch_len: int32 [16, 64], P('seq'), may hold values from 1 to 16, 256 in all within a row
- patch_owner: int32 [1024, 1], P('seq'), may hold values from 0 to 7; in each aligned block of 128 rows (0 to 127, 128 to 255, ...) at most 32 rows name the same one
- w_query: bfloat16 [4096, 4096], P('seq', 'mp'), may hold values from -0.09375 to 0.09375
Outputs:
- win_dq: bfloat16 [4096, 4096], P('seq', 'mp')
- win_dk: bfloat16 [4096, 4096], P('seq', 'mp')
- win_dv: bfloat16 [4096, 4096], P('seq', 'mp')
- patch_grads: bfloat16 [2, 2048, 4096], P(None, 'seq', 'mp')
- byte_grads: bfloat16 [4096, 4096], P('seq', 'mp')
The draws below stay inside these ranges and needn't reach their ends.
Inputs may be any that keep to these rules, and one draw needn't show every extreme that they name: `patch_len`: each row lists the byte lengths of the patches of one stored block in order; they sum to 256 and the largest is exactly 16. `patch_owner`: within each aligned block of 128 rows (the patch rows of one device) no owner is named more than 32 times, a bound that some block reaches.
All inputs are finite; a program needn't handle non-finite values.
Results may differ from the reference program's by a relative error of at most 0.017.
Values may be sent and summed in bfloat16 or wider, within the bound.
A program may use at most 128 MiB of HBM per device.

```python
import math
import jax
import jax.numpy as jnp
import numpy as np
from jax import lax

D = 4096
HEADS = 32
HD = 128
WIN = 256
LMAX = 16
BLK = 256
PB = 64
BLOCKS = 16
BYTES = 4096
PATCHES = 1024
CAP = 32
SLOTS = 2048
N_SEQ = 8
N_MP = 4


def noise_rows(key, salt, row_count, width):
    base_key = jax.random.fold_in(key, salt)
    return jax.random.truncated_normal(base_key, -6.0, 6.0, (row_count, width), jnp.float32)


def draw_win_query(key, part):
    width = HEADS * HD
    values = noise_rows(key, 31, BYTES, width)
    return values.astype(jnp.bfloat16)


def draw_win_key(key, part):
    width = HEADS * HD
    values = noise_rows(key, 32, BYTES, width)
    return values.astype(jnp.bfloat16)


def draw_cross_query(key, part):
    width = HEADS * HD
    values = noise_rows(key, 41, BYTES, width)
    return values.astype(jnp.bfloat16)


def draw_patch_key(key, part):
    width = HEADS * HD
    values = noise_rows(key, 42, PATCHES, width)
    return values.astype(jnp.bfloat16)


def shard_levels(stream_key, shape, pieces, least, largest):
    def one(dim, parts):
        steps = jax.random.uniform(jax.random.fold_in(jax.random.fold_in(stream_key, 6), dim), (parts,), jnp.float32, least / len(pieces), largest / len(pieces))
        return jnp.repeat(jnp.exp(steps), shape[dim] // parts).reshape((-1,) + (1,) * (len(shape) - dim - 1))

    level = one(*pieces[0])
    for cut in pieces[1:]:
        level = level * one(*cut)
    return level


def length_profile(amount, total, most, lean):
    weights = [(1 << 20) // math.isqrt(rank ** lean) + 1 for rank in range(2, amount + 1)]
    rest, counts = total - most - (amount - 1), [1] * (amount - 1)
    while rest > 0:
        movable = [i for i in range(amount - 1) if counts[i] < most]
        pool, left = sum([weights[i] for i in movable]), rest
        for i in movable:
            more = min(most - counts[i], max(1, left * weights[i] // pool), rest)
            counts[i] = counts[i] + more
            rest = rest - more
    return np.array([most] + counts)


def ragged(own_key, number_of, total, reach, skew):
    if number_of == 2:
        one = jax.random.randint(own_key, (), max(1, total - reach), min(reach, total - 1) + 1)
        return jnp.stack([one, total - one])
    tallies = jnp.asarray(length_profile(number_of, total, reach, skew), jnp.int32)
    pairs = (number_of - 1) // 2
    donor, sink = tallies[1:1 + 2 * pairs:2], tallies[2:2 + 2 * pairs:2]
    margin = jnp.minimum(donor - 1, reach - sink)
    passed = jax.random.randint(jax.random.fold_in(own_key, 1), (pairs,), 0, 1 << 20) % (margin + 1)
    tallies = tallies.at[1:1 + 2 * pairs:2].set(donor - passed).at[2:2 + 2 * pairs:2].set(sink + passed)
    return tallies[jax.random.permutation(jax.random.fold_in(own_key, 2), number_of)]


def shared_out(rng, own, number, rows, amount, top, limit, lean):
    sequence = jax.random.permutation(rng, amount)
    heavy_load, common = load_shares(amount, rows * top, limit, lean, True), load_shares(amount, rows * top, limit, lean, False)
    places = jnp.arange(amount)

    def named(lengths, turn):
        used = int((lengths > 0).sum())
        fixed = max(1, used // 4)
        shifted = fixed + (places - fixed + turn * (used - fixed)) % max(1, amount - fixed)
        return jnp.zeros((amount,), jnp.int32).at[sequence[jnp.where(places < fixed, places, shifted)]].set(jnp.asarray(lengths, jnp.int32))

    lengths = jnp.where(number % 4 == 0, named(heavy_load, number // 4), named(common, number - number // 4 - 1))
    mixed = jax.random.permutation(jax.random.fold_in(own, 3), amount)
    giver, receiver = mixed[0:amount // 2 * 2:2], mixed[1:amount // 2 * 2:2]
    room = jnp.minimum(lengths[giver] - 1, limit - lengths[receiver]) // 2
    room = jnp.where((giver == sequence[0]) | (receiver == sequence[0]) | (lengths[receiver] == 0), 0, jnp.maximum(room, 0))
    shifted = jax.random.randint(jax.random.fold_in(own, 4), (amount // 2,), 0, 1 << 20) % (room + 1)
    lengths = lengths.at[giver].add(-shifted).at[receiver].add(shifted)
    members = jnp.searchsorted(jnp.cumsum(lengths), jnp.arange(rows * top), side="right").astype(jnp.int32)
    grid = members.reshape(top, rows).T
    grid = grid[jax.random.permutation(jax.random.fold_in(own, 1), rows)]
    turn = jax.random.randint(jax.random.fold_in(own, 2), (rows, 1), 0, top)
    return jnp.take_along_axis(grid, (jnp.arange(top)[None, :] + turn) % top, axis=1)


def load_shares(count, total, bound, skew, full):
    weights = [(1 << 20) // math.isqrt(grade ** skew) + 1 for grade in range(1, count + 1)]
    largest = bound if full else min(bound, max(-(-total // count), total * weights[0] // sum(weights)))
    least = 1 if total - largest >= count - 1 else 0
    counts, surplus = [largest] + [least] * (count - 1), total - largest - least * (count - 1)
    while surplus > 0:
        free = [i for i in range(1, count) if counts[i] < largest] or [i for i in range(1, count) if counts[i] < bound]
        mass, remaining = sum([weights[i] for i in free]), surplus
        for i in free:
            more = min(bound - counts[i], max(1, remaining * weights[i] // mass), surplus)
            counts[i] = counts[i] + more
            surplus = surplus - more
    return np.array(counts)


def scatter_about(own_key, dims, scale, reach, shards=(), held_as=jnp.bfloat16):
    entries = scale * jax.random.normal(own_key, dims, jnp.float32)
    if shards:
        entries = entries * shard_levels(own_key, dims, shards, -0.22, 0.18)
    return jnp.clip(entries, -reach, reach).astype(held_as)


def setup_inputs(seed: int = 0) -> dict:
    key_list = jax.random.split(jax.random.key(seed), 12)
    win_query = draw_win_query(jax.random.fold_in(key_list[11], 71), 0)
    win_key = draw_win_key(jax.random.fold_in(key_list[11], 71), 0)
    win_value = scatter_about(key_list[2], (BYTES, HEADS * HD), 1.0, 6.0, ((0, 8), (1, 4)))
    win_dout = scatter_about(key_list[3], (BYTES, HEADS * HD), 4.0, 16.0, ((0, 8), (1, 4)))
    cross_query = draw_cross_query(jax.random.fold_in(key_list[11], 71), 0)
    cross_dout = scatter_about(key_list[5], (BYTES, HEADS * HD), 4.0, 16.0, ((0, 8), (1, 4)))
    patch_key = draw_patch_key(jax.random.fold_in(key_list[11], 71), 0)
    patch_value = scatter_about(key_list[7], (PATCHES, HEADS * HD), 1.0, 6.0, ((0, 8), (1, 4)))
    patch_len = jax.vmap(lambda own: ragged(own, PB, BLK, LMAX, 2))(jax.random.split(key_list[8], BLOCKS)).reshape((BLOCKS, PB)).astype(jnp.int32)
    patch_owner_keys = jax.random.split(jax.random.fold_in(key_list[9], 1), PATCHES // (2 * PB))
    patch_owner_turns = jax.random.permutation(jax.random.fold_in(key_list[9], 3), PATCHES // (2 * PB))
    patch_owner = jax.vmap(lambda own, number: shared_out(jax.random.fold_in(key_list[9], 2), own, number, 2 * PB, N_SEQ, 1, CAP, 2))(patch_owner_keys, patch_owner_turns).reshape((PATCHES, 1))
    w_query = scatter_about(key_list[10], (D, HEADS * HD), (HEADS * HD) ** -0.5, 0.09375, ((0, 8), (1, 4)))
    return dict(win_query=win_query, win_key=win_key, win_value=win_value, win_dout=win_dout, cross_query=cross_query, cross_dout=cross_dout, patch_key=patch_key, patch_value=patch_value, patch_len=patch_len, patch_owner=patch_owner, w_query=w_query)


def row_stats(scores, allowed):
    masked = jnp.where(allowed, scores, -1e+30)
    row_top = lax.optimization_barrier(jnp.max(masked, axis=-1, keepdims=True))
    row_total = lax.optimization_barrier(jnp.sum(jnp.exp(jnp.where(allowed, scores - row_top, -1e+30)), axis=-1, keepdims=True))
    return row_top + jnp.log(row_total)

def window_block(query_block, dout_block, key_ext, value_ext, tail_valid):
    window = WIN
    inv_root = 1.0 / math.sqrt(HD)
    length = query_block.shape[0]
    width = query_block.shape[1]
    head_count = width // HD
    query_heads = query_block.astype(jnp.float32).reshape(length, head_count, HD)
    dout_heads = dout_block.astype(jnp.float32).reshape(length, head_count, HD)
    key_heads = key_ext.astype(jnp.float32).reshape(length + window, head_count, HD)
    value_heads = value_ext.astype(jnp.float32).reshape(length + window, head_count, HD)
    rows_at = lax.broadcasted_iota(jnp.int32, (window, 2 * window), 0)
    cols_at = lax.broadcasted_iota(jnp.int32, (window, 2 * window), 1)
    gap = cols_at - rows_at

    def one_step(sub_step, state_in):
        dq_acc, dk_acc, dv_acc = state_in
        offset = sub_step * window
        query_sub = lax.dynamic_slice_in_dim(query_heads, offset, window, 0)
        dout_sub = lax.dynamic_slice_in_dim(dout_heads, offset, window, 0)
        key_sub = lax.dynamic_slice_in_dim(key_heads, offset, 2 * window, 0)
        value_sub = lax.dynamic_slice_in_dim(value_heads, offset, 2 * window, 0)
        allowed = ((gap >= 0) & (gap <= window) & ((cols_at + offset >= window) | tail_valid))[None]
        scores = jnp.einsum('qhd,khd->hqk', query_sub, key_sub) * inv_root
        log_total = row_stats(scores, allowed)
        prob_rows = jnp.exp(jnp.where(allowed, scores - log_total, -1e+30))
        dprobs = jnp.einsum('qhd,khd->hqk', dout_sub, value_sub)
        row_delta = lax.optimization_barrier(jnp.sum(prob_rows * dprobs, axis=-1, keepdims=True))
        grad_low = lax.optimization_barrier((prob_rows * (dprobs - row_delta) * inv_root).astype(jnp.bfloat16))
        probs_low = lax.optimization_barrier(prob_rows.astype(jnp.bfloat16))
        grad_wide = grad_low.astype(jnp.float32)
        probs_wide = probs_low.astype(jnp.float32)
        dq_sub = jnp.einsum('hqk,khd->qhd', grad_wide, key_sub)
        dk_sub = jnp.einsum('hqk,qhd->khd', grad_wide, query_sub)
        dv_sub = jnp.einsum('hqk,qhd->khd', probs_wide, dout_sub)
        dq_acc = lax.dynamic_update_slice_in_dim(dq_acc, dq_sub, offset, 0)
        dk_acc = lax.dynamic_update_slice_in_dim(dk_acc, lax.dynamic_slice_in_dim(dk_acc, offset, 2 * window, 0) + dk_sub, offset, 0)
        dv_acc = lax.dynamic_update_slice_in_dim(dv_acc, lax.dynamic_slice_in_dim(dv_acc, offset, 2 * window, 0) + dv_sub, offset, 0)
        return (dq_acc, dk_acc, dv_acc)
    start_state = (jnp.zeros((length, head_count, HD), jnp.float32), jnp.zeros((length + window, head_count, HD), jnp.float32), jnp.zeros((length + window, head_count, HD), jnp.float32))
    dq_acc, dk_acc, dv_acc = lax.fori_loop(0, length // window, one_step, start_state)
    return (dq_acc.reshape(length, width), dk_acc.reshape(length + window, width), dv_acc.reshape(length + window, width))

def cross_block(items):
    query_block, dout_block, key_rows, value_rows, length_row = items
    inv_root = 1.0 / math.sqrt(HD)
    width = query_block.shape[1]
    head_count = width // HD
    query_heads = query_block.astype(jnp.float32).reshape(BLK, head_count, HD)
    dout_heads = dout_block.astype(jnp.float32).reshape(BLK, head_count, HD)
    key_heads = key_rows.astype(jnp.float32).reshape(PB, head_count, HD)
    value_heads = value_rows.astype(jnp.float32).reshape(PB, head_count, HD)
    starts = jnp.cumsum(length_row) - length_row
    within = jnp.arange(BLK)
    allowed = (starts[None, :] <= within[:, None])[None]
    scores = jnp.einsum('qhd,khd->hqk', query_heads, key_heads) * inv_root
    log_total = row_stats(scores, allowed)
    prob_rows = jnp.exp(jnp.where(allowed, scores - log_total, -1e+30))
    dprobs = jnp.einsum('qhd,khd->hqk', dout_heads, value_heads)
    row_delta = lax.optimization_barrier(jnp.sum(prob_rows * dprobs, axis=-1, keepdims=True))
    grad_low = lax.optimization_barrier((prob_rows * (dprobs - row_delta) * inv_root).astype(jnp.bfloat16))
    probs_low = lax.optimization_barrier(prob_rows.astype(jnp.bfloat16))
    grad_wide = grad_low.astype(jnp.float32)
    probs_wide = probs_low.astype(jnp.float32)
    dq_rows = jnp.einsum('hqk,khd->qhd', grad_wide, key_heads).reshape(BLK, width).astype(jnp.bfloat16)
    dk_rows = jnp.einsum('hqk,qhd->khd', grad_wide, query_heads).reshape(PB, width).astype(jnp.bfloat16)
    dv_rows = jnp.einsum('hqk,qhd->khd', probs_wide, dout_heads).reshape(PB, width).astype(jnp.bfloat16)
    return (dq_rows, dk_rows, dv_rows)

def reference(win_query, win_key, win_value, win_dout, cross_query, cross_dout, patch_key, patch_value, patch_len, patch_owner, w_query):
    width = HEADS * HD
    seq_of_stored = np.array([row_block // 2 if row_block % 2 == 0 else BLOCKS - 1 - row_block // 2 for row_block in range(BLOCKS)])
    stored_of_seq = np.argsort(seq_of_stored)

    def to_seq(values):
        return values.reshape(BLOCKS, BLK, width)[stored_of_seq]

    def to_stored(values):
        return values[seq_of_stored].reshape(BYTES, width)
    query_seq = to_seq(win_query)
    dout_seq = to_seq(win_dout)
    key_seq = to_seq(win_key)
    value_seq = to_seq(win_value)
    zero_rim = jnp.zeros((1, WIN, width), win_key.dtype)
    key_rims = jnp.concatenate([zero_rim, key_seq[:-1, BLK - WIN:]], axis=0)
    value_rims = jnp.concatenate([zero_rim, value_seq[:-1, BLK - WIN:]], axis=0)
    rim_valid = jnp.arange(BLOCKS) > 0

    def one_block(items):
        query_block, dout_block, key_block, value_block, key_rim, value_rim, valid = items
        return window_block(query_block, dout_block, jnp.concatenate([key_rim, key_block], axis=0), jnp.concatenate([value_rim, value_block], axis=0), valid)
    dq_seq, dk_ext, dv_ext = lax.map(one_block, (query_seq, dout_seq, key_seq, value_seq, key_rims, value_rims, rim_valid))
    dk_seq = dk_ext[:, WIN:].at[:-1, BLK - WIN:].add(dk_ext[1:, :WIN])
    dv_seq = dv_ext[:, WIN:].at[:-1, BLK - WIN:].add(dv_ext[1:, :WIN])
    win_dq = to_stored(dq_seq.astype(jnp.bfloat16))
    win_dk = to_stored(dk_seq.astype(jnp.bfloat16))
    win_dv = to_stored(dv_seq.astype(jnp.bfloat16))
    cross_items = (cross_query.reshape(BLOCKS, BLK, width), cross_dout.reshape(BLOCKS, BLK, width), patch_key.reshape(BLOCKS, PB, width), patch_value.reshape(BLOCKS, PB, width), patch_len)
    dq_blocks, dk_blocks, dv_blocks = lax.map(cross_block, cross_items)
    cross_dq = dq_blocks.reshape(BYTES, width)
    patch_dk = dk_blocks.reshape(PATCHES, width)
    patch_dv = dv_blocks.reshape(PATCHES, width)
    owners = patch_owner[:, 0].reshape(N_SEQ, 2 * PB).astype(jnp.int32)
    onehot = (owners[:, :, None] == jnp.arange(N_SEQ).astype(jnp.int32)[None, None, :]).astype(jnp.int32)
    slot_rank = lax.optimization_barrier(jnp.sum(onehot * (jnp.cumsum(onehot, axis=1) - onehot), axis=2))
    slot_index = (owners * CAP + slot_rank).astype(jnp.int32)
    stacked = jnp.stack([patch_dk, patch_dv]).reshape(2, N_SEQ, 2 * PB, width)
    sources = jnp.arange(N_SEQ).astype(jnp.int32)[:, None]
    placed = jnp.zeros((2, N_SEQ, N_SEQ * CAP, width), jnp.bfloat16).at[:, sources, slot_index].set(stacked)
    patch_grads = placed.reshape(2, N_SEQ, N_SEQ, CAP, width).transpose(0, 2, 1, 3, 4).reshape(2, SLOTS, width)
    group_cols = width // N_MP

    def add_group(group, accum):
        begin = group * group_cols
        dq_group = lax.dynamic_slice_in_dim(cross_dq, begin, group_cols, 1)
        w_group = lax.dynamic_slice_in_dim(w_query, begin, group_cols, 1)
        part_low = lax.optimization_barrier(jnp.dot(dq_group, w_group.T, preferred_element_type=jnp.float32).astype(jnp.bfloat16))
        return accum + part_low.astype(jnp.float32)
    byte_sum = lax.fori_loop(0, N_MP, add_group, jnp.zeros((BYTES, D), jnp.float32))
    byte_grads = byte_sum.astype(jnp.bfloat16)
    return (win_dq, win_dk, win_dv, patch_grads, byte_grads)
```

```python
import functools
import math

import jax
import jax.numpy as jnp
from jax import lax
from jax.experimental import pallas as pl
from jax.experimental.pallas import tpu as pltpu
from jax.sharding import PartitionSpec as P

HD = 128
WIN = 256
NT = (((1,), (1,)), ((), ()))
NN = (((1,), (0,)), ((), ()))
TN = (((0,), (0,)), ((), ()))


def dot(left, right, dims):
    return lax.dot_general(left, right, dims, preferred_element_type=jnp.float32)


def attention_grads(query, dout, keys, values, allowed):
    inv_root = 1.0 / math.sqrt(HD)
    scores = jnp.where(allowed, dot(query, keys, NT) * inv_root, -1e30)
    top = jnp.max(scores, axis=-1, keepdims=True)
    weights = jnp.where(allowed, jnp.exp(scores - top), 0.0)
    probs = weights * (1.0 / jnp.sum(weights, axis=-1, keepdims=True))
    dprobs = dot(dout, values, NT)
    delta = jnp.sum(probs * dprobs, axis=-1, keepdims=True)
    grad = (probs * (dprobs - delta) * inv_root).astype(jnp.bfloat16)
    return probs.astype(jnp.bfloat16), grad


def window_kernel(
    seq_count, q_ref, k_ref, v_ref, do_ref, before_ref, after_ref,
    dq_ref, dk_ref, dv_ref, low_ref, high_ref,
):
    seq_index = lax.axis_index("seq")
    is_last = seq_index == seq_count - 1
    rows_at = lax.broadcasted_iota(jnp.int32, (WIN, 2 * WIN), 0)
    cols_at = lax.broadcasted_iota(jnp.int32, (WIN, 2 * WIN), 1)
    gap = cols_at - rows_at
    inside = (gap >= 0) & (gap <= WIN)
    first_col = jnp.where(seq_index > 0, 0, WIN)
    low, high = slice(0, WIN), slice(WIN, 2 * WIN)

    def part(rows, rim_key, rim_value, allowed):
        query, dout = q_ref[rows, :], do_ref[rows, :]
        keys = jnp.concatenate([rim_key, k_ref[rows, :]], axis=0)
        values = jnp.concatenate([rim_value, v_ref[rows, :]], axis=0)
        probs, grad = attention_grads(query, dout, keys, values, allowed)
        dq_ref[rows, :] = dot(grad, keys, NN).astype(jnp.bfloat16)
        return dot(grad, query, TN), dot(probs, dout, TN)

    low_dk, low_dv = part(low, before_ref[0], before_ref[1], inside & (cols_at >= first_col))
    high_dk, high_dv = part(
        high,
        jnp.where(is_last, k_ref[low, :], after_ref[0]),
        jnp.where(is_last, v_ref[low, :], after_ref[1]),
        inside,
    )
    low_ref[0] = low_dk[:WIN].astype(jnp.bfloat16)
    low_ref[1] = low_dv[:WIN].astype(jnp.bfloat16)
    high_ref[0] = high_dk[:WIN].astype(jnp.bfloat16)
    high_ref[1] = high_dv[:WIN].astype(jnp.bfloat16)
    dk_ref[low, :] = (low_dk[WIN:] + jnp.where(is_last, high_dk[:WIN], 0.0)).astype(jnp.bfloat16)
    dv_ref[low, :] = (low_dv[WIN:] + jnp.where(is_last, high_dv[:WIN], 0.0)).astype(jnp.bfloat16)
    dk_ref[high, :] = high_dk[WIN:].astype(jnp.bfloat16)
    dv_ref[high, :] = high_dv[WIN:].astype(jnp.bfloat16)


def window_call(seq_count, query, key, value, dout, before, after):
    rows, width = query.shape
    heads = width // HD
    own = pl.BlockSpec((rows, HD), lambda h: (0, h))
    rim = pl.BlockSpec((2, WIN, HD), lambda h: (0, 0, h))
    full = jax.ShapeDtypeStruct((rows, width), jnp.bfloat16)
    rims = jax.ShapeDtypeStruct((2, WIN, width), jnp.bfloat16)
    return pl.pallas_call(
        functools.partial(window_kernel, seq_count),
        grid=(heads,),
        in_specs=[own, own, own, own, rim, rim],
        out_specs=[own, own, own, rim, rim],
        out_shape=[full, full, full, rims, rims],
        compiler_params=pltpu.CompilerParams(vmem_limit_bytes=32 << 20),
        cost_estimate=pl.CostEstimate(
            flops=heads * 10 * rows * 2 * WIN * HD,
            bytes_accessed=26 * rows * width,
            transcendentals=heads * rows * 2 * WIN,
        ),
        name="window",
    )(query, key, value, dout, before, after)


def cross_kernel(
    cap, q_ref, do_ref, k_ref, v_ref, len_ref, owner_col_ref, owner_row_ref, dq_ref, slots_ref
):
    rows, patches = q_ref.shape[0], k_ref.shape[0]
    block_rows, per_block = rows // 2, patches // 2
    earlier_at = lax.broadcasted_iota(jnp.int32, (patches, patches), 0)
    later_at = lax.broadcasted_iota(jnp.int32, (patches, patches), 1)
    before = earlier_at < later_at
    same_block = (earlier_at >= per_block) == (later_at >= per_block)
    starts = jnp.sum(jnp.where(before & same_block, len_ref[...], 0), axis=0, keepdims=True)
    same_owner = owner_col_ref[...] == owner_row_ref[...]
    rank = jnp.sum(jnp.where(before & same_owner, 1, 0), axis=0, keepdims=True)
    slot = owner_row_ref[...] * cap + rank
    rows_at = lax.broadcasted_iota(jnp.int32, (rows, patches), 0)
    cols_at = lax.broadcasted_iota(jnp.int32, (rows, patches), 1)
    upper_row, upper_col = rows_at >= block_rows, cols_at >= per_block
    within = jnp.where(upper_row, rows_at - block_rows, rows_at)
    allowed = (starts <= within) & (upper_row == upper_col)
    query, dout, keys, values = q_ref[...], do_ref[...], k_ref[...], v_ref[...]
    probs, grad = attention_grads(query, dout, keys, values, allowed)
    dq_ref[...] = dot(grad, keys, NN).astype(jnp.bfloat16)
    patch_dk = dot(grad, query, TN).astype(jnp.bfloat16)
    patch_dv = dot(probs, dout, TN).astype(jnp.bfloat16)
    slots = slots_ref.shape[1]
    chosen = lax.broadcasted_iota(jnp.int32, (slots, patches), 0) == slot
    selector = jnp.where(chosen, 1.0, 0.0).astype(jnp.bfloat16)
    slots_ref[0] = dot(selector, patch_dk, NN).astype(jnp.bfloat16)
    slots_ref[1] = dot(selector, patch_dv, NN).astype(jnp.bfloat16)


def cross_call(cap, slots, query, dout, key, value, lengths, owner):
    rows, width = query.shape
    patches = key.shape[0]
    heads = width // HD
    own = pl.BlockSpec((rows, HD), lambda h: (0, h))
    patch = pl.BlockSpec((patches, HD), lambda h: (0, h))
    column = pl.BlockSpec((patches, 1), lambda h: (0, 0))
    line = pl.BlockSpec((1, patches), lambda h: (0, 0))
    return pl.pallas_call(
        functools.partial(cross_kernel, cap),
        grid=(heads,),
        in_specs=[own, own, patch, patch, column, column, line],
        out_specs=[own, pl.BlockSpec((2, slots, HD), lambda h: (0, 0, h))],
        out_shape=[
            jax.ShapeDtypeStruct((rows, width), jnp.bfloat16),
            jax.ShapeDtypeStruct((2, slots, width), jnp.bfloat16),
        ],
        compiler_params=pltpu.CompilerParams(vmem_limit_bytes=32 << 20),
        cost_estimate=pl.CostEstimate(
            flops=heads * 12 * rows * patches * HD,
            bytes_accessed=8 * rows * width,
            transcendentals=heads * rows * patches,
        ),
        name="cross",
    )(query, dout, key, value, lengths.reshape(patches, 1), owner, owner.reshape(1, patches))


def target(place, me, count):
    if count != 4:
        return place
    row, core = me // 2, me % 2
    return (row if place % 2 else 1 - row) * 2 + (1 - core if place < 2 else core)


def parts_kernel(count, per_plane, *refs):
    dq_ref, w_refs = refs[0], refs[1 : 2 * count]
    send_ref, keep_ref, held, sems = refs[2 * count :]
    step = pl.program_id(0)
    plane = lax.axis_index("seq") // per_plane
    me = lax.axis_index("mp")

    @pl.when(step == 0)
    def _():
        for place in range(count):
            gap = target(place, me, count) - plane
            for index, w_ref in enumerate(w_refs):

                @pl.when(gap == index - (count - 1))
                def _(w_ref=w_ref, place=place):
                    pltpu.make_async_copy(w_ref, held.at[place], sems.at[place]).start()

    pltpu.make_async_copy(w_refs[0], held.at[step], sems.at[step]).wait()
    product = dot(dq_ref[...], held[step], NT).astype(jnp.bfloat16)

    @pl.when(step < count // 2)
    def _():
        send_ref[0] = product

    @pl.when(step >= count // 2)
    def _():
        keep_ref[0] = product


def parts_call(count, per_plane, dq, blocks):
    rows, width = dq.shape
    depth = blocks[0].shape[0]
    half = count // 2
    shape = jax.ShapeDtypeStruct((half, rows, depth), jnp.bfloat16)
    return pl.pallas_call(
        functools.partial(parts_kernel, count, per_plane),
        grid=(count,),
        in_specs=[pl.BlockSpec((rows, width), lambda j: (0, 0))]
        + [pl.BlockSpec(memory_space=pl.ANY)] * len(blocks),
        out_specs=[
            pl.BlockSpec((1, rows, depth), lambda j: (jnp.minimum(j, half - 1), 0, 0)),
            pl.BlockSpec((1, rows, depth), lambda j: (jnp.maximum(j - half, 0), 0, 0)),
        ],
        out_shape=[shape, shape],
        scratch_shapes=[
            pltpu.VMEM((count, depth, width), jnp.bfloat16),
            pltpu.SemaphoreType.DMA((count,)),
        ],
        compiler_params=pltpu.CompilerParams(vmem_limit_bytes=32 << 20),
        cost_estimate=pl.CostEstimate(
            flops=2 * rows * width * depth * count,
            bytes_accessed=2 * (rows * width + count * depth * (rows + width)),
            transcendentals=0,
        ),
        name="parts",
    )(dq, *blocks)


def gather_planes(block, planes, per_plane):
    seq_count = planes * per_plane
    up, down = {0: block}, {0: block}
    for hop in range(1, planes):
        up_route = [
            (s, s + per_plane)
            for s in range(seq_count - per_plane)
            if s // per_plane >= hop - 1
        ]
        down_route = [(seq_count - 1 - a, seq_count - 1 - b) for a, b in up_route]
        up[hop] = lax.ppermute(up[hop - 1], "seq", up_route)
        down[hop] = lax.ppermute(down[hop - 1], "seq", down_route)
    return [up[hop] for hop in range(planes - 1, 0, -1)] + [down[hop] for hop in range(planes)]


def shifted(block, distance, count):
    route = [(i - distance, i) for i in range(count) if 0 <= i - distance < count]
    return lax.ppermute(block, "seq", route)


def turned(block, distance, count, per_plane):
    route = [
        (s, s - s % per_plane + (s % per_plane + distance) % per_plane) for s in range(count)
    ]
    return lax.ppermute(block, "seq", route)


def summed(send, keep, count):
    if count != 4:
        parts = jnp.concatenate([send, keep], axis=0)
        return lax.psum_scatter(parts, "mp", scatter_dimension=0, tiled=True)[0]
    arrived = lax.ppermute(send, "mp", [(m, m ^ 1) for m in range(count)])
    wide = arrived.astype(jnp.float32) + keep.astype(jnp.float32)
    across = lax.ppermute(wide[0].astype(jnp.bfloat16), "mp", [(m, m ^ 2) for m in range(count)])
    return (wide[1] + across.astype(jnp.float32)).astype(jnp.bfloat16)


def local(
    win_query,
    win_key,
    win_value,
    win_dout,
    cross_query,
    cross_dout,
    patch_key,
    patch_value,
    patch_len,
    patch_owner,
    w_query,
):
    seq_count, mp_count = lax.axis_size("seq"), lax.axis_size("mp")
    per_plane = seq_count // mp_count
    planes = mp_count
    column = lax.axis_index("seq") % per_plane
    width = win_query.shape[1]
    patch_rows = patch_key.shape[0]

    blocks = gather_planes(w_query, planes, per_plane)
    low_rim = jnp.stack([win_key[:WIN], win_value[:WIN]])
    high_rim = jnp.stack([win_key[WIN:], win_value[WIN:]])
    before = shifted(low_rim, 1, seq_count)
    after = shifted(high_rim, -1, seq_count)

    cap = max(2, 2 * (patch_rows // seq_count))
    cross_dq, slots = cross_call(
        cap, seq_count * cap, cross_query, cross_dout, patch_key, patch_value, patch_len, patch_owner
    )
    all_dq = [cross_dq] + [
        turned(cross_dq, r, seq_count, per_plane) for r in range(1, per_plane)
    ]
    arrived = lax.all_to_all(
        slots.reshape(2, seq_count, cap, width), "seq", split_axis=1, concat_axis=1, tiled=True
    )
    patch_grads = arrived.reshape(2, seq_count * cap, width)

    win_dq, own_dk, own_dv, low_send, high_send = window_call(
        seq_count, win_query, win_key, win_value, win_dout, before, after
    )
    low_back = shifted(low_send, -1, seq_count)
    high_back = shifted(high_send, 1, seq_count)

    def joined(own, index):
        back = jnp.concatenate([low_back[index], high_back[index]], axis=0)
        return (own.astype(jnp.float32) + back.astype(jnp.float32)).astype(jnp.bfloat16)

    win_dk, win_dv = joined(own_dk, 0), joined(own_dv, 1)

    near = [None] * per_plane
    for r in range(per_plane - 1, -1, -1):
        send, keep = parts_call(planes, per_plane, all_dq[r], blocks)
        total = summed(send, keep, mp_count)
        near[r] = turned(total, -r, seq_count, per_plane) if r else total
    pieces = []
    for j in range(per_plane):
        piece = near[j]
        for x in range(1, per_plane):
            piece = jnp.where(column == x, near[(j - x) % per_plane], piece)
        pieces.append(piece)
    byte_grads = jnp.concatenate(pieces, axis=1)
    return (win_dq, win_dk, win_dv, patch_grads, byte_grads)


def solution(mesh):
    in_specs = (P("seq", "mp"),) * 8 + (P("seq", None),) * 2 + (P("seq", "mp"),)
    out_specs = (P("seq", "mp"),) * 3 + (P(None, "seq", "mp"), P("seq", "mp"))
    return jax.shard_map(local, mesh=mesh, in_specs=in_specs, out_specs=out_specs, check_vma=False)
```

```python
import functools
import math

import jax
import jax.numpy as jnp
from jax import lax
from jax.experimental import pallas as pl
from jax.experimental.pallas import tpu as pltpu
from jax.sharding import PartitionSpec as P

HD = 128
WIN = 256
NT = (((1,), (1,)), ((), ()))
NN = (((1,), (0,)), ((), ()))
TN = (((0,), (0,)), ((), ()))


def dot(left, right, dims):
    return lax.dot_general(left, right, dims, preferred_element_type=jnp.float32)


def attention_grads(query, dout, keys, values, allowed):
    inv_root = 1.0 / math.sqrt(HD)
    scores = jnp.where(allowed, dot(query, keys, NT) * inv_root, -1e30)
    top = jnp.max(scores, axis=-1, keepdims=True)
    weights = jnp.where(allowed, jnp.exp(scores - top), 0.0)
    probs = weights * (1.0 / jnp.sum(weights, axis=-1, keepdims=True))
    dprobs = dot(dout, values, NT)
    delta = jnp.sum(probs * dprobs, axis=-1, keepdims=True)
    grad = (probs * (dprobs - delta) * inv_root).astype(jnp.bfloat16)
    return probs.astype(jnp.bfloat16), grad


def window_kernel(
    seq_count, q_ref, k_ref, v_ref, do_ref, before_ref, after_ref,
    dq_ref, dk_ref, dv_ref, low_dk_ref, high_dk_ref, low_dv_ref, high_dv_ref,
):
    seq_index = lax.axis_index("seq")
    is_last = seq_index == seq_count - 1
    rows_at = lax.broadcasted_iota(jnp.int32, (WIN, 2 * WIN), 0)
    cols_at = lax.broadcasted_iota(jnp.int32, (WIN, 2 * WIN), 1)
    gap = cols_at - rows_at
    inside = (gap >= 0) & (gap <= WIN)
    first_col = jnp.where(seq_index > 0, 0, WIN)
    low, high = slice(0, WIN), slice(WIN, 2 * WIN)

    def part(rows, rim_key, rim_value, allowed):
        query, dout = q_ref[rows, :], do_ref[rows, :]
        keys = jnp.concatenate([rim_key, k_ref[rows, :]], axis=0)
        values = jnp.concatenate([rim_value, v_ref[rows, :]], axis=0)
        probs, grad = attention_grads(query, dout, keys, values, allowed)
        dq_ref[rows, :] = dot(grad, keys, NN).astype(jnp.bfloat16)
        return dot(grad, query, TN), dot(probs, dout, TN)

    low_dk, low_dv = part(low, before_ref[0], before_ref[1], inside & (cols_at >= first_col))
    high_dk, high_dv = part(
        high,
        jnp.where(is_last, k_ref[low, :], after_ref[0]),
        jnp.where(is_last, v_ref[low, :], after_ref[1]),
        inside,
    )
    low_dk_ref[...] = low_dk[:WIN].astype(jnp.bfloat16)
    low_dv_ref[...] = low_dv[:WIN].astype(jnp.bfloat16)
    high_dk_ref[...] = high_dk[:WIN].astype(jnp.bfloat16)
    high_dv_ref[...] = high_dv[:WIN].astype(jnp.bfloat16)
    dk_ref[low, :] = (low_dk[WIN:] + jnp.where(is_last, high_dk[:WIN], 0.0)).astype(jnp.bfloat16)
    dv_ref[low, :] = (low_dv[WIN:] + jnp.where(is_last, high_dv[:WIN], 0.0)).astype(jnp.bfloat16)
    dk_ref[high, :] = high_dk[WIN:].astype(jnp.bfloat16)
    dv_ref[high, :] = high_dv[WIN:].astype(jnp.bfloat16)


def window_call(seq_count, query, key, value, dout, before, after):
    rows, width = query.shape
    heads = width // HD
    own = pl.BlockSpec((rows, HD), lambda h: (0, h))
    rim = pl.BlockSpec((2, WIN, HD), lambda h: (0, 0, h))
    full = jax.ShapeDtypeStruct((rows, width), jnp.bfloat16)
    sent = pl.BlockSpec((WIN, HD), lambda h: (0, h))
    rims = jax.ShapeDtypeStruct((WIN, width), jnp.bfloat16)
    return pl.pallas_call(
        functools.partial(window_kernel, seq_count),
        grid=(heads,),
        in_specs=[own, own, own, own, rim, rim],
        out_specs=[own, own, own] + [sent] * 4,
        out_shape=[full, full, full] + [rims] * 4,
        compiler_params=pltpu.CompilerParams(vmem_limit_bytes=60 << 20),
        cost_estimate=pl.CostEstimate(
            flops=heads * 10 * rows * 2 * WIN * HD,
            bytes_accessed=26 * rows * width,
            transcendentals=heads * rows * 2 * WIN,
        ),
        name="window",
    )(query, key, value, dout, before, after)


def join_kernel(own_ref, low_ref, high_ref, out_ref):
    for part, back in enumerate((low_ref, high_ref)):
        rows = slice(part * WIN, (part + 1) * WIN)
        total = own_ref[rows, :].astype(jnp.float32) + back[...].astype(jnp.float32)
        out_ref[rows, :] = total.astype(jnp.bfloat16)


def join_call(own, low_back, high_back):
    rows, width = own.shape
    tile = 2 * HD
    whole = pl.BlockSpec((rows, tile), lambda h: (0, h))
    rim = pl.BlockSpec((WIN, tile), lambda h: (0, h))
    return pl.pallas_call(
        join_kernel,
        grid=(width // tile,),
        in_specs=[whole, rim, rim],
        out_specs=whole,
        out_shape=jax.ShapeDtypeStruct((rows, width), jnp.bfloat16),
        compiler_params=pltpu.CompilerParams(vmem_limit_bytes=60 << 20),
        cost_estimate=pl.CostEstimate(
            flops=rows * width, bytes_accessed=6 * rows * width, transcendentals=0
        ),
        name="join",
    )(own, low_back, high_back)


def cross_kernel(
    cap, q_ref, do_ref, k_ref, v_ref, len_ref, owner_col_ref, owner_row_ref, dq_ref, slots_ref
):
    rows, patches = q_ref.shape[0], k_ref.shape[0]
    block_rows, per_block = rows // 2, patches // 2
    earlier_at = lax.broadcasted_iota(jnp.int32, (patches, patches), 0)
    later_at = lax.broadcasted_iota(jnp.int32, (patches, patches), 1)
    before = earlier_at < later_at
    same_block = (earlier_at >= per_block) == (later_at >= per_block)
    starts = jnp.sum(jnp.where(before & same_block, len_ref[...], 0), axis=0, keepdims=True)
    same_owner = owner_col_ref[...] == owner_row_ref[...]
    rank = jnp.sum(jnp.where(before & same_owner, 1, 0), axis=0, keepdims=True)
    slot = owner_row_ref[...] * cap + rank
    rows_at = lax.broadcasted_iota(jnp.int32, (rows, patches), 0)
    cols_at = lax.broadcasted_iota(jnp.int32, (rows, patches), 1)
    upper_row, upper_col = rows_at >= block_rows, cols_at >= per_block
    within = jnp.where(upper_row, rows_at - block_rows, rows_at)
    allowed = (starts <= within) & (upper_row == upper_col)
    query, dout, keys, values = q_ref[...], do_ref[...], k_ref[...], v_ref[...]
    probs, grad = attention_grads(query, dout, keys, values, allowed)
    dq_ref[...] = dot(grad, keys, NN).astype(jnp.bfloat16)
    patch_dk = dot(grad, query, TN).astype(jnp.bfloat16)
    patch_dv = dot(probs, dout, TN).astype(jnp.bfloat16)
    slots = slots_ref.shape[1]
    chosen = lax.broadcasted_iota(jnp.int32, (slots, patches), 0) == slot
    selector = jnp.where(chosen, 1.0, 0.0).astype(jnp.bfloat16)
    slots_ref[0] = dot(selector, patch_dk, NN).astype(jnp.bfloat16)
    slots_ref[1] = dot(selector, patch_dv, NN).astype(jnp.bfloat16)


def cross_call(cap, slots, query, dout, key, value, lengths, owner):
    rows, width = query.shape
    patches = key.shape[0]
    heads = width // HD
    own = pl.BlockSpec((rows, HD), lambda h: (0, h))
    patch = pl.BlockSpec((patches, HD), lambda h: (0, h))
    column = pl.BlockSpec((patches, 1), lambda h: (0, 0))
    line = pl.BlockSpec((1, patches), lambda h: (0, 0))
    return pl.pallas_call(
        functools.partial(cross_kernel, cap),
        grid=(heads,),
        in_specs=[own, own, patch, patch, column, column, line],
        out_specs=[own, pl.BlockSpec((2, slots, HD), lambda h: (0, 0, h))],
        out_shape=[
            jax.ShapeDtypeStruct((rows, width), jnp.bfloat16),
            jax.ShapeDtypeStruct((2, slots, width), jnp.bfloat16),
        ],
        compiler_params=pltpu.CompilerParams(vmem_limit_bytes=60 << 20),
        cost_estimate=pl.CostEstimate(
            flops=heads * 12 * rows * patches * HD,
            bytes_accessed=8 * rows * width,
            transcendentals=heads * rows * patches,
        ),
        name="cross",
    )(query, dout, key, value, lengths.reshape(patches, 1), owner, owner.reshape(1, patches))


def target(place, me, count):
    if count != 4:
        return place
    row, core = me // 2, me % 2
    return (row if place % 2 else 1 - row) * 2 + (1 - core if place < 2 else core)


def parts_kernel(count, per_plane, *refs):
    dq_ref, w_refs = refs[0], refs[1 : 2 * count]
    send_ref, keep_ref, held, sems = refs[2 * count :]
    step = pl.program_id(0)
    plane = lax.axis_index("seq") // per_plane
    me = lax.axis_index("mp")

    @pl.when(step == 0)
    def _():
        for place in range(count):
            gap = target(place, me, count) - plane
            for index, w_ref in enumerate(w_refs):

                @pl.when(gap == index - (count - 1))
                def _(w_ref=w_ref, place=place):
                    pltpu.make_async_copy(w_ref, held.at[place], sems.at[place]).start()

    pltpu.make_async_copy(w_refs[0], held.at[step], sems.at[step]).wait()
    product = dot(dq_ref[...], held[step], NT).astype(jnp.bfloat16)

    @pl.when(step < count // 2)
    def _():
        send_ref[0] = product

    @pl.when(step >= count // 2)
    def _():
        keep_ref[0] = product


def parts_call(count, per_plane, dq, blocks):
    rows, width = dq.shape
    depth = blocks[0].shape[0]
    half = count // 2
    shape = jax.ShapeDtypeStruct((half, rows, depth), jnp.bfloat16)
    return pl.pallas_call(
        functools.partial(parts_kernel, count, per_plane),
        grid=(count,),
        in_specs=[pl.BlockSpec((rows, width), lambda j: (0, 0))]
        + [pl.BlockSpec(memory_space=pl.ANY)] * len(blocks),
        out_specs=[
            pl.BlockSpec((1, rows, depth), lambda j: (jnp.minimum(j, half - 1), 0, 0)),
            pl.BlockSpec((1, rows, depth), lambda j: (jnp.maximum(j - half, 0), 0, 0)),
        ],
        out_shape=[shape, shape],
        scratch_shapes=[
            pltpu.VMEM((count, depth, width), jnp.bfloat16),
            pltpu.SemaphoreType.DMA((count,)),
        ],
        compiler_params=pltpu.CompilerParams(vmem_limit_bytes=60 << 20),
        cost_estimate=pl.CostEstimate(
            flops=2 * rows * width * depth * count,
            bytes_accessed=2 * (rows * width + count * depth * (rows + width)),
            transcendentals=0,
        ),
        name="parts",
    )(dq, *blocks)


def plane_routes(planes, per_plane, hop):
    seq_count = planes * per_plane
    up = [
        (s, s + per_plane) for s in range(seq_count - per_plane) if s // per_plane >= hop - 1
    ]
    return up, [(seq_count - 1 - a, seq_count - 1 - b) for a, b in up]


def plane_step(up, down, planes, per_plane, hop):
    up_route, down_route = plane_routes(planes, per_plane, hop)
    return lax.ppermute(up, "seq", up_route), lax.ppermute(down, "seq", down_route)


def shifted(block, distance, count):
    route = [(i - distance, i) for i in range(count) if 0 <= i - distance < count]
    return lax.ppermute(block, "seq", route)


def turned(block, distance, count, per_plane):
    route = [
        (s, s - s % per_plane + (s % per_plane + distance) % per_plane) for s in range(count)
    ]
    return lax.ppermute(block, "seq", route)


def summed(send, keep, count):
    if count != 4:
        parts = jnp.concatenate([send, keep], axis=0)
        return lax.psum_scatter(parts, "mp", scatter_dimension=0, tiled=True)[0]
    arrived = lax.ppermute(send, "mp", [(m, m ^ 1) for m in range(count)])
    wide = arrived.astype(jnp.float32) + keep.astype(jnp.float32)
    across = lax.ppermute(wide[0].astype(jnp.bfloat16), "mp", [(m, m ^ 2) for m in range(count)])
    return (wide[1] + across.astype(jnp.float32)).astype(jnp.bfloat16)


def local(
    win_query,
    win_key,
    win_value,
    win_dout,
    cross_query,
    cross_dout,
    patch_key,
    patch_value,
    patch_len,
    patch_owner,
    w_query,
):
    seq_count, mp_count = lax.axis_size("seq"), lax.axis_size("mp")
    per_plane = seq_count // mp_count
    planes = mp_count
    column = lax.axis_index("seq") % per_plane
    width = win_query.shape[1]
    patch_rows = patch_key.shape[0]

    up, down = {0: w_query}, {0: w_query}
    up[1], down[1] = plane_step(w_query, w_query, planes, per_plane, 1)
    low_rim = jnp.stack([win_key[:WIN], win_value[:WIN]])
    high_rim = jnp.stack([win_key[WIN:], win_value[WIN:]])

    patch_len, low_rim, high_rim = lax.optimization_barrier((patch_len, low_rim, high_rim))
    before = shifted(low_rim, 1, seq_count)
    after = shifted(high_rim, -1, seq_count)
    cap = max(2, 2 * (patch_rows // seq_count))
    cross_dq, slots = cross_call(
        cap, seq_count * cap, cross_query, cross_dout, patch_key, patch_value, patch_len, patch_owner
    )
    all_dq = [cross_dq] + [
        turned(cross_dq, r, seq_count, per_plane) for r in range(1, per_plane)
    ]
    up[1], down[1], slots, before, after = lax.optimization_barrier(
        (up[1], down[1], slots, before, after)
    )
    up[2], down[2] = plane_step(up[1], down[1], planes, per_plane, 2)
    up[2], down[2], *swapped = lax.optimization_barrier((up[2], down[2], *all_dq[1:]))
    all_dq[1:] = swapped
    for hop in range(3, planes):
        up[hop], down[hop] = plane_step(up[hop - 1], down[hop - 1], planes, per_plane, hop)
    win_dq, own_dk, own_dv, low_dk, high_dk, low_dv, high_dv = window_call(
        seq_count, win_query, win_key, win_value, win_dout, before, after
    )
    slots, low_dk, high_dk = lax.optimization_barrier((slots, low_dk, high_dk))
    low_dk_back = shifted(low_dk, -1, seq_count)
    high_dk_back = shifted(high_dk, 1, seq_count)
    arrived = lax.all_to_all(
        slots.reshape(2, seq_count, cap, width), "seq", split_axis=1, concat_axis=1, tiled=True
    )
    patch_grads = arrived.reshape(2, seq_count * cap, width)
    win_dk = join_call(own_dk, low_dk_back, high_dk_back)

    last = planes - 1
    patch_grads, win_dk, low_dv, high_dv, up[last], down[last] = lax.optimization_barrier(
        (patch_grads, win_dk, low_dv, high_dv, up[last], down[last])
    )
    low_dv_back = shifted(low_dv, -1, seq_count)
    high_dv_back = shifted(high_dv, 1, seq_count)
    blocks = [up[hop] for hop in range(last, 0, -1)] + [down[hop] for hop in range(planes)]

    near = [None] * per_plane
    for r in range(per_plane - 1, -1, -1):
        send, keep = parts_call(planes, per_plane, all_dq[r], blocks)
        total = summed(send, keep, mp_count)
        near[r] = turned(total, -r, seq_count, per_plane) if r else total
    low_dv_back, high_dv_back, near[0] = lax.optimization_barrier(
        (low_dv_back, high_dv_back, near[0])
    )
    win_dv = join_call(own_dv, low_dv_back, high_dv_back)
    pieces = []
    for j in range(per_plane):
        piece = near[j]
        for x in range(1, per_plane):
            piece = jnp.where(column == x, near[(j - x) % per_plane], piece)
        pieces.append(piece)
    byte_grads = jnp.concatenate(pieces, axis=1)
    return (win_dq, win_dk, win_dv, patch_grads, byte_grads)


def solution(mesh):
    in_specs = (P("seq", "mp"),) * 8 + (P("seq", None),) * 2 + (P("seq", "mp"),)
    out_specs = (P("seq", "mp"),) * 3 + (P(None, "seq", "mp"), P("seq", "mp"))
    return jax.shard_map(local, mesh=mesh, in_specs=in_specs, out_specs=out_specs, check_vma=False)
```

```python
import functools
import math

import jax
import jax.numpy as jnp
from jax import lax
from jax.experimental import pallas as pl
from jax.experimental.pallas import tpu as pltpu
from jax.sharding import PartitionSpec as P

HD = 128
WIN = 256
NT = (((1,), (1,)), ((), ()))
NN = (((1,), (0,)), ((), ()))
TN = (((0,), (0,)), ((), ()))


def dot(left, right, dims):
    return lax.dot_general(left, right, dims, preferred_element_type=jnp.float32)


def attention_grads(query, dout, keys, values, allowed):
    inv_root = 1.0 / math.sqrt(HD)
    scores = jnp.where(allowed, dot(query, keys, NT) * inv_root, -1e30)
    top = jnp.max(scores, axis=-1, keepdims=True)
    weights = jnp.where(allowed, jnp.exp(scores - top), 0.0)
    probs = weights * (1.0 / jnp.sum(weights, axis=-1, keepdims=True))
    dprobs = dot(dout, values, NT)
    delta = jnp.sum(probs * dprobs, axis=-1, keepdims=True)
    grad = (probs * (dprobs - delta) * inv_root).astype(jnp.bfloat16)
    return probs.astype(jnp.bfloat16), grad


def window_kernel(
    seq_count, q_ref, k_ref, v_ref, do_ref, before_ref, after_ref,
    dq_ref, dk_ref, dv_ref, low_ref, high_ref,
):
    seq_index = lax.axis_index("seq")
    is_last = seq_index == seq_count - 1
    rows_at = lax.broadcasted_iota(jnp.int32, (WIN, 2 * WIN), 0)
    cols_at = lax.broadcasted_iota(jnp.int32, (WIN, 2 * WIN), 1)
    gap = cols_at - rows_at
    inside = (gap >= 0) & (gap <= WIN)
    first_col = jnp.where(seq_index > 0, 0, WIN)
    low, high = slice(0, WIN), slice(WIN, 2 * WIN)

    def part(rows, rim_key, rim_value, allowed):
        query, dout = q_ref[rows, :], do_ref[rows, :]
        keys = jnp.concatenate([rim_key, k_ref[rows, :]], axis=0)
        values = jnp.concatenate([rim_value, v_ref[rows, :]], axis=0)
        probs, grad = attention_grads(query, dout, keys, values, allowed)
        dq_ref[rows, :] = dot(grad, keys, NN).astype(jnp.bfloat16)
        return dot(grad, query, TN), dot(probs, dout, TN)

    low_dk, low_dv = part(low, before_ref[0], before_ref[1], inside & (cols_at >= first_col))
    high_dk, high_dv = part(
        high,
        jnp.where(is_last, k_ref[low, :], after_ref[0]),
        jnp.where(is_last, v_ref[low, :], after_ref[1]),
        inside,
    )
    low_ref[0] = low_dk[:WIN].astype(jnp.bfloat16)
    low_ref[1] = low_dv[:WIN].astype(jnp.bfloat16)
    high_ref[0] = high_dk[:WIN].astype(jnp.bfloat16)
    high_ref[1] = high_dv[:WIN].astype(jnp.bfloat16)
    dk_ref[low, :] = (low_dk[WIN:] + jnp.where(is_last, high_dk[:WIN], 0.0)).astype(jnp.bfloat16)
    dv_ref[low, :] = (low_dv[WIN:] + jnp.where(is_last, high_dv[:WIN], 0.0)).astype(jnp.bfloat16)
    dk_ref[high, :] = high_dk[WIN:].astype(jnp.bfloat16)
    dv_ref[high, :] = high_dv[WIN:].astype(jnp.bfloat16)


def window_call(seq_count, query, key, value, dout, before, after):
    rows, width = query.shape
    heads = width // HD
    own = pl.BlockSpec((rows, HD), lambda h: (0, h))
    rim = pl.BlockSpec((2, WIN, HD), lambda h: (0, 0, h))
    full = jax.ShapeDtypeStruct((rows, width), jnp.bfloat16)
    rims = jax.ShapeDtypeStruct((2, WIN, width), jnp.bfloat16)
    return pl.pallas_call(
        functools.partial(window_kernel, seq_count),
        grid=(heads,),
        in_specs=[own, own, own, own, rim, rim],
        out_specs=[own, own, own, rim, rim],
        out_shape=[full, full, full, rims, rims],
        compiler_params=pltpu.CompilerParams(vmem_limit_bytes=60 << 20),
        cost_estimate=pl.CostEstimate(
            flops=heads * 10 * rows * 2 * WIN * HD,
            bytes_accessed=60 * rows * width,
            transcendentals=heads * rows * 2 * WIN,
        ),
        name="window",
    )(query, key, value, dout, before, after)


def join_kernel(dk_ref, dv_ref, low_ref, high_ref, out_dk_ref, out_dv_ref):
    for index, (own, out) in enumerate(((dk_ref, out_dk_ref), (dv_ref, out_dv_ref))):
        for part, back in enumerate((low_ref, high_ref)):
            rows = slice(part * WIN, (part + 1) * WIN)
            total = own[rows, :].astype(jnp.float32) + back[index].astype(jnp.float32)
            out[rows, :] = total.astype(jnp.bfloat16)


def join_call(own_dk, own_dv, low_back, high_back):
    rows, width = own_dk.shape
    tile = 2 * HD
    own = pl.BlockSpec((rows, tile), lambda h: (0, h))
    rim = pl.BlockSpec((2, WIN, tile), lambda h: (0, 0, h))
    full = jax.ShapeDtypeStruct((rows, width), jnp.bfloat16)
    return pl.pallas_call(
        join_kernel,
        grid=(width // tile,),
        in_specs=[own, own, rim, rim],
        out_specs=[own, own],
        out_shape=[full, full],
        compiler_params=pltpu.CompilerParams(vmem_limit_bytes=60 << 20),
        cost_estimate=pl.CostEstimate(
            flops=2 * rows * width, bytes_accessed=12 * rows * width, transcendentals=0
        ),
        name="join",
    )(own_dk, own_dv, low_back, high_back)


def cross_kernel(
    cap, q_ref, do_ref, k_ref, v_ref, len_ref, owner_col_ref, owner_row_ref, dq_ref, slots_ref
):
    rows, patches = q_ref.shape[0], k_ref.shape[0]
    block_rows, per_block = rows // 2, patches // 2
    earlier_at = lax.broadcasted_iota(jnp.int32, (patches, patches), 0)
    later_at = lax.broadcasted_iota(jnp.int32, (patches, patches), 1)
    before = earlier_at < later_at
    same_block = (earlier_at >= per_block) == (later_at >= per_block)
    starts = jnp.sum(jnp.where(before & same_block, len_ref[...], 0), axis=0, keepdims=True)
    same_owner = owner_col_ref[...] == owner_row_ref[...]
    rank = jnp.sum(jnp.where(before & same_owner, 1, 0), axis=0, keepdims=True)
    slot = owner_row_ref[...] * cap + rank
    rows_at = lax.broadcasted_iota(jnp.int32, (rows, patches), 0)
    cols_at = lax.broadcasted_iota(jnp.int32, (rows, patches), 1)
    upper_row, upper_col = rows_at >= block_rows, cols_at >= per_block
    within = jnp.where(upper_row, rows_at - block_rows, rows_at)
    allowed = (starts <= within) & (upper_row == upper_col)
    query, dout, keys, values = q_ref[...], do_ref[...], k_ref[...], v_ref[...]
    probs, grad = attention_grads(query, dout, keys, values, allowed)
    dq_ref[...] = dot(grad, keys, NN).astype(jnp.bfloat16)
    patch_dk = dot(grad, query, TN).astype(jnp.bfloat16)
    patch_dv = dot(probs, dout, TN).astype(jnp.bfloat16)
    slots = slots_ref.shape[1]
    chosen = lax.broadcasted_iota(jnp.int32, (slots, patches), 0) == slot
    selector = jnp.where(chosen, 1.0, 0.0).astype(jnp.bfloat16)
    slots_ref[0] = dot(selector, patch_dk, NN).astype(jnp.bfloat16)
    slots_ref[1] = dot(selector, patch_dv, NN).astype(jnp.bfloat16)


def cross_call(cap, slots, query, dout, key, value, lengths, owner):
    rows, width = query.shape
    patches = key.shape[0]
    heads = width // HD
    own = pl.BlockSpec((rows, HD), lambda h: (0, h))
    patch = pl.BlockSpec((patches, HD), lambda h: (0, h))
    column = pl.BlockSpec((patches, 1), lambda h: (0, 0))
    line = pl.BlockSpec((1, patches), lambda h: (0, 0))
    return pl.pallas_call(
        functools.partial(cross_kernel, cap),
        grid=(heads,),
        in_specs=[own, own, patch, patch, column, column, line],
        out_specs=[own, pl.BlockSpec((2, slots, HD), lambda h: (0, 0, h))],
        out_shape=[
            jax.ShapeDtypeStruct((rows, width), jnp.bfloat16),
            jax.ShapeDtypeStruct((2, slots, width), jnp.bfloat16),
        ],
        compiler_params=pltpu.CompilerParams(vmem_limit_bytes=60 << 20),
        cost_estimate=pl.CostEstimate(
            flops=heads * 12 * rows * patches * HD,
            bytes_accessed=8 * rows * width,
            transcendentals=heads * rows * patches,
        ),
        name="cross",
    )(query, dout, key, value, lengths.reshape(patches, 1), owner, owner.reshape(1, patches))


def target(place, me, count):
    if count != 4:
        return place
    row, core = me // 2, me % 2
    return (row if place % 2 else 1 - row) * 2 + (1 - core if place < 2 else core)


def parts_kernel(count, per_plane, *refs):
    dq_ref, w_refs = refs[0], refs[1 : 2 * count]
    send_ref, keep_ref, held, sems = refs[2 * count :]
    step = pl.program_id(0)
    plane = lax.axis_index("seq") // per_plane
    me = lax.axis_index("mp")

    @pl.when(step == 0)
    def _():
        for place in range(count):
            gap = target(place, me, count) - plane
            for index, w_ref in enumerate(w_refs):

                @pl.when(gap == index - (count - 1))
                def _(w_ref=w_ref, place=place):
                    pltpu.make_async_copy(w_ref, held.at[place], sems.at[place]).start()

    pltpu.make_async_copy(w_refs[0], held.at[step], sems.at[step]).wait()
    product = dot(dq_ref[...], held[step], NT).astype(jnp.bfloat16)

    @pl.when(step < count // 2)
    def _():
        send_ref[0] = product

    @pl.when(step >= count // 2)
    def _():
        keep_ref[0] = product


def parts_call(count, per_plane, dq, blocks):
    rows, width = dq.shape
    depth = blocks[0].shape[0]
    half = count // 2
    shape = jax.ShapeDtypeStruct((half, rows, depth), jnp.bfloat16)
    return pl.pallas_call(
        functools.partial(parts_kernel, count, per_plane),
        grid=(count,),
        in_specs=[pl.BlockSpec((rows, width), lambda j: (0, 0))]
        + [pl.BlockSpec(memory_space=pl.ANY)] * len(blocks),
        out_specs=[
            pl.BlockSpec((1, rows, depth), lambda j: (jnp.minimum(j, half - 1), 0, 0)),
            pl.BlockSpec((1, rows, depth), lambda j: (jnp.maximum(j - half, 0), 0, 0)),
        ],
        out_shape=[shape, shape],
        scratch_shapes=[
            pltpu.VMEM((count, depth, width), jnp.bfloat16),
            pltpu.SemaphoreType.DMA((count,)),
        ],
        compiler_params=pltpu.CompilerParams(vmem_limit_bytes=32 << 20),
        cost_estimate=pl.CostEstimate(
            flops=rows * width * depth,
            bytes_accessed=2 * rows * width,
            transcendentals=0,
        ),
        name="parts",
    )(dq, *blocks)


def plane_routes(planes, per_plane, hop):
    seq_count = planes * per_plane
    up = [
        (s, s + per_plane) for s in range(seq_count - per_plane) if s // per_plane >= hop - 1
    ]
    return up, [(seq_count - 1 - a, seq_count - 1 - b) for a, b in up]


def plane_step(up, down, planes, per_plane, hop):
    up_route, down_route = plane_routes(planes, per_plane, hop)
    return lax.ppermute(up, "seq", up_route), lax.ppermute(down, "seq", down_route)


def shifted(block, distance, count):
    route = [(i - distance, i) for i in range(count) if 0 <= i - distance < count]
    return lax.ppermute(block, "seq", route)


def turned(block, distance, count, per_plane):
    route = [
        (s, s - s % per_plane + (s % per_plane + distance) % per_plane) for s in range(count)
    ]
    return lax.ppermute(block, "seq", route)


def summed(send, keep, count):
    if count != 4:
        parts = jnp.concatenate([send, keep], axis=0)
        return lax.psum_scatter(parts, "mp", scatter_dimension=0, tiled=True)[0]
    arrived = lax.ppermute(send, "mp", [(m, m ^ 1) for m in range(count)])
    wide = arrived.astype(jnp.float32) + keep.astype(jnp.float32)
    across = lax.ppermute(wide[0].astype(jnp.bfloat16), "mp", [(m, m ^ 2) for m in range(count)])
    return (wide[1] + across.astype(jnp.float32)).astype(jnp.bfloat16)


def local(
    win_query,
    win_key,
    win_value,
    win_dout,
    cross_query,
    cross_dout,
    patch_key,
    patch_value,
    patch_len,
    patch_owner,
    w_query,
):
    seq_count, mp_count = lax.axis_size("seq"), lax.axis_size("mp")
    per_plane = seq_count // mp_count
    planes = mp_count
    column = lax.axis_index("seq") % per_plane
    width = win_query.shape[1]
    patch_rows = patch_key.shape[0]

    up, down = {0: w_query}, {0: w_query}
    up[1], down[1] = plane_step(w_query, w_query, planes, per_plane, 1)
    cap = max(2, 2 * (patch_rows // seq_count))
    cross_dq, slots = cross_call(
        cap, seq_count * cap, cross_query, cross_dout, patch_key, patch_value, patch_len, patch_owner
    )
    all_dq = [cross_dq] + [
        turned(cross_dq, r, seq_count, per_plane) for r in range(1, per_plane)
    ]
    up[1], down[1], slots = lax.optimization_barrier((up[1], down[1], slots))
    up[2], down[2] = plane_step(up[1], down[1], planes, per_plane, 2)
    slots, up[1], down[1] = lax.optimization_barrier((slots, up[1], down[1]))
    arrived = lax.all_to_all(
        slots.reshape(2, seq_count, cap, width), "seq", split_axis=1, concat_axis=1, tiled=True
    )
    patch_grads = arrived.reshape(2, seq_count * cap, width)

    low_rim = jnp.stack([win_key[:WIN], win_value[:WIN]])
    high_rim = jnp.stack([win_key[WIN:], win_value[WIN:]])
    before = shifted(low_rim, 1, seq_count)
    after = shifted(high_rim, -1, seq_count)
    up[2], down[2], before, after, patch_grads, *all_dq = lax.optimization_barrier(
        (up[2], down[2], before, after, patch_grads, *all_dq)
    )
    for hop in range(3, planes):
        up[hop], down[hop] = plane_step(up[hop - 1], down[hop - 1], planes, per_plane, hop)
    win_dq, own_dk, own_dv, low_send, high_send = window_call(
        seq_count, win_query, win_key, win_value, win_dout, before, after
    )
    low_back = shifted(low_send, -1, seq_count)
    high_back = shifted(high_send, 1, seq_count)
    last = planes - 1
    up[last], down[last], win_dq = lax.optimization_barrier((up[last], down[last], win_dq))
    blocks = [up[hop] for hop in range(last, 0, -1)] + [down[hop] for hop in range(planes)]

    near = [None] * per_plane
    for r in range(per_plane - 1, -1, -1):
        send, keep = parts_call(planes, per_plane, all_dq[r], blocks)
        if r == per_plane - 1:
            send, low_back, high_back = lax.optimization_barrier((send, low_back, high_back))
        total = summed(send, keep, mp_count)
        near[r] = turned(total, -r, seq_count, per_plane) if r else total
    win_dk, win_dv = join_call(own_dk, own_dv, low_back, high_back)
    pieces = []
    for j in range(per_plane):
        piece = near[j]
        for x in range(1, per_plane):
            piece = jnp.where(column == x, near[(j - x) % per_plane], piece)
        pieces.append(piece)
    byte_grads = jnp.concatenate(pieces, axis=1)
    return (win_dq, win_dk, win_dv, patch_grads, byte_grads)


def solution(mesh):
    in_specs = (P("seq", "mp"),) * 8 + (P("seq", None),) * 2 + (P("seq", "mp"),)
    out_specs = (P("seq", "mp"),) * 3 + (P(None, "seq", "mp"), P("seq", "mp"))
    return jax.shard_map(local, mesh=mesh, in_specs=in_specs, out_specs=out_specs, check_vma=False)
```

```python
import functools
import math

import jax
import jax.numpy as jnp
from jax import lax
from jax.experimental import pallas as pl
from jax.experimental.pallas import tpu as pltpu
from jax.sharding import PartitionSpec as P

HD = 128
WIN = 256
NT = (((1,), (1,)), ((), ()))
NN = (((1,), (0,)), ((), ()))
TN = (((0,), (0,)), ((), ()))


def dot(left, right, dims):
    return lax.dot_general(left, right, dims, preferred_element_type=jnp.float32)


def attention_grads(query, dout, keys, values, allowed):
    inv_root = 1.0 / math.sqrt(HD)
    scores = jnp.where(allowed, dot(query, keys, NT) * inv_root, -1e30)
    top = jnp.max(scores, axis=-1, keepdims=True)
    weights = jnp.where(allowed, jnp.exp(scores - top), 0.0)
    probs = weights * (1.0 / jnp.sum(weights, axis=-1, keepdims=True))
    dprobs = dot(dout, values, NT)
    delta = jnp.sum(probs * dprobs, axis=-1, keepdims=True)
    grad = (probs * (dprobs - delta) * inv_root).astype(jnp.bfloat16)
    return probs.astype(jnp.bfloat16), grad


def window_kernel(
    seq_count, q_ref, k_ref, v_ref, do_ref, before_ref, after_ref,
    dq_ref, dk_ref, dv_ref, low_ref, high_ref,
):
    seq_index = lax.axis_index("seq")
    is_last = seq_index == seq_count - 1
    rows_at = lax.broadcasted_iota(jnp.int32, (WIN, 2 * WIN), 0)
    cols_at = lax.broadcasted_iota(jnp.int32, (WIN, 2 * WIN), 1)
    gap = cols_at - rows_at
    inside = (gap >= 0) & (gap <= WIN)
    first_col = jnp.where(seq_index > 0, 0, WIN)
    low, high = slice(0, WIN), slice(WIN, 2 * WIN)

    def part(rows, rim_key, rim_value, allowed):
        query, dout = q_ref[rows, :], do_ref[rows, :]
        keys = jnp.concatenate([rim_key, k_ref[rows, :]], axis=0)
        values = jnp.concatenate([rim_value, v_ref[rows, :]], axis=0)
        probs, grad = attention_grads(query, dout, keys, values, allowed)
        dq_ref[rows, :] = dot(grad, keys, NN).astype(jnp.bfloat16)
        return dot(grad, query, TN), dot(probs, dout, TN)

    low_dk, low_dv = part(low, before_ref[0], before_ref[1], inside & (cols_at >= first_col))
    high_dk, high_dv = part(
        high,
        jnp.where(is_last, k_ref[low, :], after_ref[0]),
        jnp.where(is_last, v_ref[low, :], after_ref[1]),
        inside,
    )
    low_ref[0] = low_dk[:WIN].astype(jnp.bfloat16)
    low_ref[1] = low_dv[:WIN].astype(jnp.bfloat16)
    high_ref[0] = high_dk[:WIN].astype(jnp.bfloat16)
    high_ref[1] = high_dv[:WIN].astype(jnp.bfloat16)
    dk_ref[low, :] = (low_dk[WIN:] + jnp.where(is_last, high_dk[:WIN], 0.0)).astype(jnp.bfloat16)
    dv_ref[low, :] = (low_dv[WIN:] + jnp.where(is_last, high_dv[:WIN], 0.0)).astype(jnp.bfloat16)
    dk_ref[high, :] = high_dk[WIN:].astype(jnp.bfloat16)
    dv_ref[high, :] = high_dv[WIN:].astype(jnp.bfloat16)


def window_call(seq_count, query, key, value, dout, before, after):
    rows, width = query.shape
    heads = width // HD
    own = pl.BlockSpec((rows, HD), lambda h: (0, h))
    rim = pl.BlockSpec((2, WIN, HD), lambda h: (0, 0, h))
    full = jax.ShapeDtypeStruct((rows, width), jnp.bfloat16)
    rims = jax.ShapeDtypeStruct((2, WIN, width), jnp.bfloat16)
    return pl.pallas_call(
        functools.partial(window_kernel, seq_count),
        grid=(heads,),
        in_specs=[own, own, own, own, rim, rim],
        out_specs=[own, own, own, rim, rim],
        out_shape=[full, full, full, rims, rims],
        compiler_params=pltpu.CompilerParams(vmem_limit_bytes=60 << 20),
        cost_estimate=pl.CostEstimate(
            flops=heads * 10 * rows * 2 * WIN * HD,
            bytes_accessed=60 * rows * width,
            transcendentals=heads * rows * 2 * WIN,
        ),
        name="window",
    )(query, key, value, dout, before, after)


def join_kernel(dk_ref, dv_ref, low_ref, high_ref, out_dk_ref, out_dv_ref):
    for index, (own, out) in enumerate(((dk_ref, out_dk_ref), (dv_ref, out_dv_ref))):
        for part, back in enumerate((low_ref, high_ref)):
            rows = slice(part * WIN, (part + 1) * WIN)
            total = own[rows, :].astype(jnp.float32) + back[index].astype(jnp.float32)
            out[rows, :] = total.astype(jnp.bfloat16)


def join_call(own_dk, own_dv, low_back, high_back):
    rows, width = own_dk.shape
    tile = 2 * HD
    own = pl.BlockSpec((rows, tile), lambda h: (0, h))
    rim = pl.BlockSpec((2, WIN, tile), lambda h: (0, 0, h))
    full = jax.ShapeDtypeStruct((rows, width), jnp.bfloat16)
    return pl.pallas_call(
        join_kernel,
        grid=(width // tile,),
        in_specs=[own, own, rim, rim],
        out_specs=[own, own],
        out_shape=[full, full],
        compiler_params=pltpu.CompilerParams(vmem_limit_bytes=60 << 20),
        cost_estimate=pl.CostEstimate(
            flops=2 * rows * width, bytes_accessed=12 * rows * width, transcendentals=0
        ),
        name="join",
    )(own_dk, own_dv, low_back, high_back)


def cross_kernel(
    cap, q_ref, do_ref, k_ref, v_ref, len_ref, owner_col_ref, owner_row_ref, dq_ref, slots_ref
):
    rows, patches = q_ref.shape[0], k_ref.shape[0]
    block_rows, per_block = rows // 2, patches // 2
    earlier_at = lax.broadcasted_iota(jnp.int32, (patches, patches), 0)
    later_at = lax.broadcasted_iota(jnp.int32, (patches, patches), 1)
    before = earlier_at < later_at
    same_block = (earlier_at >= per_block) == (later_at >= per_block)
    starts = jnp.sum(jnp.where(before & same_block, len_ref[...], 0), axis=0, keepdims=True)
    same_owner = owner_col_ref[...] == owner_row_ref[...]
    rank = jnp.sum(jnp.where(before & same_owner, 1, 0), axis=0, keepdims=True)
    slot = owner_row_ref[...] * cap + rank
    rows_at = lax.broadcasted_iota(jnp.int32, (rows, patches), 0)
    cols_at = lax.broadcasted_iota(jnp.int32, (rows, patches), 1)
    upper_row, upper_col = rows_at >= block_rows, cols_at >= per_block
    within = jnp.where(upper_row, rows_at - block_rows, rows_at)
    allowed = (starts <= within) & (upper_row == upper_col)
    query, dout, keys, values = q_ref[...], do_ref[...], k_ref[...], v_ref[...]
    probs, grad = attention_grads(query, dout, keys, values, allowed)
    dq_ref[...] = dot(grad, keys, NN).astype(jnp.bfloat16)
    patch_dk = dot(grad, query, TN).astype(jnp.bfloat16)
    patch_dv = dot(probs, dout, TN).astype(jnp.bfloat16)
    slots = slots_ref.shape[1]
    chosen = lax.broadcasted_iota(jnp.int32, (slots, patches), 0) == slot
    selector = jnp.where(chosen, 1.0, 0.0).astype(jnp.bfloat16)
    slots_ref[0] = dot(selector, patch_dk, NN).astype(jnp.bfloat16)
    slots_ref[1] = dot(selector, patch_dv, NN).astype(jnp.bfloat16)


def cross_call(cap, slots, query, dout, key, value, lengths, owner):
    rows, width = query.shape
    patches = key.shape[0]
    heads = width // HD
    own = pl.BlockSpec((rows, HD), lambda h: (0, h))
    patch = pl.BlockSpec((patches, HD), lambda h: (0, h))
    column = pl.BlockSpec((patches, 1), lambda h: (0, 0))
    line = pl.BlockSpec((1, patches), lambda h: (0, 0))
    return pl.pallas_call(
        functools.partial(cross_kernel, cap),
        grid=(heads,),
        in_specs=[own, own, patch, patch, column, column, line],
        out_specs=[own, pl.BlockSpec((2, slots, HD), lambda h: (0, 0, h))],
        out_shape=[
            jax.ShapeDtypeStruct((rows, width), jnp.bfloat16),
            jax.ShapeDtypeStruct((2, slots, width), jnp.bfloat16),
        ],
        compiler_params=pltpu.CompilerParams(vmem_limit_bytes=60 << 20),
        cost_estimate=pl.CostEstimate(
            flops=heads * 12 * rows * patches * HD,
            bytes_accessed=8 * rows * width,
            transcendentals=heads * rows * patches,
        ),
        name="cross",
    )(query, dout, key, value, lengths.reshape(patches, 1), owner, owner.reshape(1, patches))


def target(place, me, count):
    if count != 4:
        return place
    row, core = me // 2, me % 2
    return (row if place % 2 else 1 - row) * 2 + (1 - core if place < 2 else core)


def parts_kernel(count, per_plane, *refs):
    dq_ref, w_refs = refs[0], refs[1 : 2 * count]
    send_ref, keep_ref, held, sems = refs[2 * count :]
    step = pl.program_id(0)
    plane = lax.axis_index("seq") // per_plane
    me = lax.axis_index("mp")

    @pl.when(step == 0)
    def _():
        for place in range(count):
            gap = target(place, me, count) - plane
            for index, w_ref in enumerate(w_refs):

                @pl.when(gap == index - (count - 1))
                def _(w_ref=w_ref, place=place):
                    pltpu.make_async_copy(w_ref, held.at[place], sems.at[place]).start()

    pltpu.make_async_copy(w_refs[0], held.at[step], sems.at[step]).wait()
    product = dot(dq_ref[...], held[step], NT).astype(jnp.bfloat16)

    @pl.when(step < count // 2)
    def _():
        send_ref[0] = product

    @pl.when(step >= count // 2)
    def _():
        keep_ref[0] = product


def parts_call(count, per_plane, dq, blocks):
    rows, width = dq.shape
    depth = blocks[0].shape[0]
    half = count // 2
    shape = jax.ShapeDtypeStruct((half, rows, depth), jnp.bfloat16)
    return pl.pallas_call(
        functools.partial(parts_kernel, count, per_plane),
        grid=(count,),
        in_specs=[pl.BlockSpec((rows, width), lambda j: (0, 0))]
        + [pl.BlockSpec(memory_space=pl.ANY)] * len(blocks),
        out_specs=[
            pl.BlockSpec((1, rows, depth), lambda j: (jnp.minimum(j, half - 1), 0, 0)),
            pl.BlockSpec((1, rows, depth), lambda j: (jnp.maximum(j - half, 0), 0, 0)),
        ],
        out_shape=[shape, shape],
        scratch_shapes=[
            pltpu.VMEM((count, depth, width), jnp.bfloat16),
            pltpu.SemaphoreType.DMA((count,)),
        ],
        compiler_params=pltpu.CompilerParams(vmem_limit_bytes=32 << 20),
        cost_estimate=pl.CostEstimate(
            flops=rows * width * depth,
            bytes_accessed=2 * rows * width,
            transcendentals=0,
        ),
        name="parts",
    )(dq, *blocks)


def plane_routes(planes, per_plane, hop):
    seq_count = planes * per_plane
    up = [
        (s, s + per_plane) for s in range(seq_count - per_plane) if s // per_plane >= hop - 1
    ]
    return up, [(seq_count - 1 - a, seq_count - 1 - b) for a, b in up]


def plane_step(up, down, planes, per_plane, hop):
    up_route, down_route = plane_routes(planes, per_plane, hop)
    return lax.ppermute(up, "seq", up_route), lax.ppermute(down, "seq", down_route)


def shifted(block, distance, count):
    route = [(i - distance, i) for i in range(count) if 0 <= i - distance < count]
    return lax.ppermute(block, "seq", route)


def turned(block, distance, count, per_plane):
    route = [
        (s, s - s % per_plane + (s % per_plane + distance) % per_plane) for s in range(count)
    ]
    return lax.ppermute(block, "seq", route)


def summed(send, keep, count):
    if count != 4:
        parts = jnp.concatenate([send, keep], axis=0)
        return lax.psum_scatter(parts, "mp", scatter_dimension=0, tiled=True)[0]
    arrived = lax.ppermute(send, "mp", [(m, m ^ 1) for m in range(count)])
    wide = arrived.astype(jnp.float32) + keep.astype(jnp.float32)
    across = lax.ppermute(wide[0].astype(jnp.bfloat16), "mp", [(m, m ^ 2) for m in range(count)])
    return (wide[1] + across.astype(jnp.float32)).astype(jnp.bfloat16)


def local(
    win_query,
    win_key,
    win_value,
    win_dout,
    cross_query,
    cross_dout,
    patch_key,
    patch_value,
    patch_len,
    patch_owner,
    w_query,
):
    seq_count, mp_count = lax.axis_size("seq"), lax.axis_size("mp")
    per_plane = seq_count // mp_count
    planes = mp_count
    column = lax.axis_index("seq") % per_plane
    width = win_query.shape[1]
    patch_rows = patch_key.shape[0]

    low_rim = jnp.stack([win_key[:WIN], win_value[:WIN]])
    high_rim = jnp.stack([win_key[WIN:], win_value[WIN:]])
    patch_len, low_rim, high_rim = lax.optimization_barrier((patch_len, low_rim, high_rim))
    before = shifted(low_rim, 1, seq_count)
    after = shifted(high_rim, -1, seq_count)
    up, down = {0: w_query}, {0: w_query}
    up[1], down[1] = plane_step(w_query, w_query, planes, per_plane, 1)
    cap = max(2, 2 * (patch_rows // seq_count))
    cross_dq, slots = cross_call(
        cap, seq_count * cap, cross_query, cross_dout, patch_key, patch_value, patch_len, patch_owner
    )
    all_dq = [cross_dq] + [
        turned(cross_dq, r, seq_count, per_plane) for r in range(1, per_plane)
    ]
    up[1], down[1], slots, before, after = lax.optimization_barrier(
        (up[1], down[1], slots, before, after)
    )
    up[2], down[2] = plane_step(up[1], down[1], planes, per_plane, 2)
    win_dq, own_dk, own_dv, low_send, high_send = window_call(
        seq_count, win_query, win_key, win_value, win_dout, before, after
    )
    low_back = shifted(low_send, -1, seq_count)
    high_back = shifted(high_send, 1, seq_count)
    up[2], down[2], win_dq, *all_dq = lax.optimization_barrier(
        (up[2], down[2], win_dq, *all_dq)
    )
    for hop in range(3, planes):
        up[hop], down[hop] = plane_step(up[hop - 1], down[hop - 1], planes, per_plane, hop)
    slots, win_dq = lax.optimization_barrier((slots, win_dq))
    arrived = lax.all_to_all(
        slots.reshape(2, seq_count, cap, width), "seq", split_axis=1, concat_axis=1, tiled=True
    )
    patch_grads = arrived.reshape(2, seq_count * cap, width)
    last = planes - 1
    up[last], down[last], patch_grads = lax.optimization_barrier(
        (up[last], down[last], patch_grads)
    )
    blocks = [up[hop] for hop in range(last, 0, -1)] + [down[hop] for hop in range(planes)]

    near = [None] * per_plane
    for r in range(per_plane - 1, -1, -1):
        if r == 0:
            all_dq[0], low_back, high_back = lax.optimization_barrier(
                (all_dq[0], low_back, high_back)
            )
        send, keep = parts_call(planes, per_plane, all_dq[r], blocks)
        total = summed(send, keep, mp_count)
        near[r] = turned(total, -r, seq_count, per_plane) if r else total
    win_dk, win_dv = join_call(own_dk, own_dv, low_back, high_back)
    pieces = []
    for j in range(per_plane):
        piece = near[j]
        for x in range(1, per_plane):
            piece = jnp.where(column == x, near[(j - x) % per_plane], piece)
        pieces.append(piece)
    byte_grads = jnp.concatenate(pieces, axis=1)
    return (win_dq, win_dk, win_dv, patch_grads, byte_grads)


def solution(mesh):
    in_specs = (P("seq", "mp"),) * 8 + (P("seq", None),) * 2 + (P("seq", "mp"),)
    out_specs = (P("seq", "mp"),) * 3 + (P(None, "seq", "mp"), P("seq", "mp"))
    return jax.shard_map(local, mesh=mesh, in_specs=in_specs, out_specs=out_specs, check_vma=False)
```

```python
import functools
import math

import jax
import jax.numpy as jnp
from jax import lax
from jax.experimental import pallas as pl
from jax.experimental.pallas import tpu as pltpu
from jax.sharding import PartitionSpec as P

HD = 128
WIN = 256
NT = (((1,), (1,)), ((), ()))
NN = (((1,), (0,)), ((), ()))
TN = (((0,), (0,)), ((), ()))


def dot(left, right, dims):
    return lax.dot_general(left, right, dims, preferred_element_type=jnp.float32)


def attention_grads(query, dout, keys, values, allowed):
    inv_root = 1.0 / math.sqrt(HD)
    scores = jnp.where(allowed, dot(query, keys, NT) * inv_root, -1e30)
    top = jnp.max(scores, axis=-1, keepdims=True)
    weights = jnp.where(allowed, jnp.exp(scores - top), 0.0)
    probs = weights * (1.0 / jnp.sum(weights, axis=-1, keepdims=True))
    dprobs = dot(dout, values, NT)
    delta = jnp.sum(probs * dprobs, axis=-1, keepdims=True)
    grad = (probs * (dprobs - delta) * inv_root).astype(jnp.bfloat16)
    return probs.astype(jnp.bfloat16), grad


def window_kernel(
    seq_count, q_ref, k_ref, v_ref, do_ref, before_ref, after_ref,
    dq_ref, dk_ref, dv_ref, low_ref, high_ref,
):
    seq_index = lax.axis_index("seq")
    is_last = seq_index == seq_count - 1
    rows_at = lax.broadcasted_iota(jnp.int32, (WIN, 2 * WIN), 0)
    cols_at = lax.broadcasted_iota(jnp.int32, (WIN, 2 * WIN), 1)
    gap = cols_at - rows_at
    inside = (gap >= 0) & (gap <= WIN)
    first_col = jnp.where(seq_index > 0, 0, WIN)
    low, high = slice(0, WIN), slice(WIN, 2 * WIN)

    def part(rows, rim_key, rim_value, allowed):
        query, dout = q_ref[rows, :], do_ref[rows, :]
        keys = jnp.concatenate([rim_key, k_ref[rows, :]], axis=0)
        values = jnp.concatenate([rim_value, v_ref[rows, :]], axis=0)
        probs, grad = attention_grads(query, dout, keys, values, allowed)
        dq_ref[rows, :] = dot(grad, keys, NN).astype(jnp.bfloat16)
        return dot(grad, query, TN), dot(probs, dout, TN)

    low_dk, low_dv = part(low, before_ref[0], before_ref[1], inside & (cols_at >= first_col))
    high_dk, high_dv = part(
        high,
        jnp.where(is_last, k_ref[low, :], after_ref[0]),
        jnp.where(is_last, v_ref[low, :], after_ref[1]),
        inside,
    )
    low_ref[0] = low_dk[:WIN].astype(jnp.bfloat16)
    low_ref[1] = low_dv[:WIN].astype(jnp.bfloat16)
    high_ref[0] = high_dk[:WIN].astype(jnp.bfloat16)
    high_ref[1] = high_dv[:WIN].astype(jnp.bfloat16)
    dk_ref[low, :] = (low_dk[WIN:] + jnp.where(is_last, high_dk[:WIN], 0.0)).astype(jnp.bfloat16)
    dv_ref[low, :] = (low_dv[WIN:] + jnp.where(is_last, high_dv[:WIN], 0.0)).astype(jnp.bfloat16)
    dk_ref[high, :] = high_dk[WIN:].astype(jnp.bfloat16)
    dv_ref[high, :] = high_dv[WIN:].astype(jnp.bfloat16)


def window_call(seq_count, query, key, value, dout, before, after):
    rows, width = query.shape
    heads = width // HD
    own = pl.BlockSpec((rows, HD), lambda h: (0, h))
    rim = pl.BlockSpec((2, WIN, HD), lambda h: (0, 0, h))
    full = jax.ShapeDtypeStruct((rows, width), jnp.bfloat16)
    rims = jax.ShapeDtypeStruct((2, WIN, width), jnp.bfloat16)
    return pl.pallas_call(
        functools.partial(window_kernel, seq_count),
        grid=(heads,),
        in_specs=[own, own, own, own, rim, rim],
        out_specs=[own, own, own, rim, rim],
        out_shape=[full, full, full, rims, rims],
        compiler_params=pltpu.CompilerParams(vmem_limit_bytes=60 << 20),
        cost_estimate=pl.CostEstimate(
            flops=heads * 10 * rows * 2 * WIN * HD,
            bytes_accessed=60 * rows * width,
            transcendentals=heads * rows * 2 * WIN,
        ),
        name="window",
    )(query, key, value, dout, before, after)


def join_kernel(dk_ref, dv_ref, low_ref, high_ref, out_dk_ref, out_dv_ref):
    for index, (own, out) in enumerate(((dk_ref, out_dk_ref), (dv_ref, out_dv_ref))):
        for part, back in enumerate((low_ref, high_ref)):
            rows = slice(part * WIN, (part + 1) * WIN)
            total = own[rows, :].astype(jnp.float32) + back[index].astype(jnp.float32)
            out[rows, :] = total.astype(jnp.bfloat16)


def join_call(own_dk, own_dv, low_back, high_back):
    rows, width = own_dk.shape
    tile = 2 * HD
    own = pl.BlockSpec((rows, tile), lambda h: (0, h))
    rim = pl.BlockSpec((2, WIN, tile), lambda h: (0, 0, h))
    full = jax.ShapeDtypeStruct((rows, width), jnp.bfloat16)
    return pl.pallas_call(
        join_kernel,
        grid=(width // tile,),
        in_specs=[own, own, rim, rim],
        out_specs=[own, own],
        out_shape=[full, full],
        compiler_params=pltpu.CompilerParams(vmem_limit_bytes=60 << 20),
        cost_estimate=pl.CostEstimate(
            flops=2 * rows * width, bytes_accessed=12 * rows * width, transcendentals=0
        ),
        name="join",
    )(own_dk, own_dv, low_back, high_back)


def cross_kernel(
    cap, q_ref, do_ref, k_ref, v_ref, len_ref, owner_col_ref, owner_row_ref, dq_ref, slots_ref
):
    rows, patches = q_ref.shape[0], k_ref.shape[0]
    block_rows, per_block = rows // 2, patches // 2
    earlier_at = lax.broadcasted_iota(jnp.int32, (patches, patches), 0)
    later_at = lax.broadcasted_iota(jnp.int32, (patches, patches), 1)
    before = earlier_at < later_at
    same_block = (earlier_at >= per_block) == (later_at >= per_block)
    starts = jnp.sum(jnp.where(before & same_block, len_ref[...], 0), axis=0, keepdims=True)
    same_owner = owner_col_ref[...] == owner_row_ref[...]
    rank = jnp.sum(jnp.where(before & same_owner, 1, 0), axis=0, keepdims=True)
    slot = owner_row_ref[...] * cap + rank
    rows_at = lax.broadcasted_iota(jnp.int32, (rows, patches), 0)
    cols_at = lax.broadcasted_iota(jnp.int32, (rows, patches), 1)
    upper_row, upper_col = rows_at >= block_rows, cols_at >= per_block
    within = jnp.where(upper_row, rows_at - block_rows, rows_at)
    allowed = (starts <= within) & (upper_row == upper_col)
    query, dout, keys, values = q_ref[...], do_ref[...], k_ref[...], v_ref[...]
    probs, grad = attention_grads(query, dout, keys, values, allowed)
    dq_ref[...] = dot(grad, keys, NN).astype(jnp.bfloat16)
    patch_dk = dot(grad, query, TN).astype(jnp.bfloat16)
    patch_dv = dot(probs, dout, TN).astype(jnp.bfloat16)
    slots = slots_ref.shape[1]
    chosen = lax.broadcasted_iota(jnp.int32, (slots, patches), 0) == slot
    selector = jnp.where(chosen, 1.0, 0.0).astype(jnp.bfloat16)
    slots_ref[0] = dot(selector, patch_dk, NN).astype(jnp.bfloat16)
    slots_ref[1] = dot(selector, patch_dv, NN).astype(jnp.bfloat16)


def cross_call(cap, slots, query, dout, key, value, lengths, owner):
    rows, width = query.shape
    patches = key.shape[0]
    heads = width // HD
    own = pl.BlockSpec((rows, HD), lambda h: (0, h))
    patch = pl.BlockSpec((patches, HD), lambda h: (0, h))
    column = pl.BlockSpec((patches, 1), lambda h: (0, 0))
    line = pl.BlockSpec((1, patches), lambda h: (0, 0))
    return pl.pallas_call(
        functools.partial(cross_kernel, cap),
        grid=(heads,),
        in_specs=[own, own, patch, patch, column, column, line],
        out_specs=[own, pl.BlockSpec((2, slots, HD), lambda h: (0, 0, h))],
        out_shape=[
            jax.ShapeDtypeStruct((rows, width), jnp.bfloat16),
            jax.ShapeDtypeStruct((2, slots, width), jnp.bfloat16),
        ],
        compiler_params=pltpu.CompilerParams(vmem_limit_bytes=60 << 20),
        cost_estimate=pl.CostEstimate(
            flops=heads * 12 * rows * patches * HD,
            bytes_accessed=8 * rows * width,
            transcendentals=heads * rows * patches,
        ),
        name="cross",
    )(query, dout, key, value, lengths.reshape(patches, 1), owner, owner.reshape(1, patches))


def target(place, me, count):
    if count != 4:
        return place
    row, core = me // 2, me % 2
    return (row if place % 2 else 1 - row) * 2 + (1 - core if place < 2 else core)


def parts_kernel(count, per_plane, *refs):
    dq_ref, w_refs = refs[0], refs[1 : 2 * count]
    send_ref, keep_ref, held, sems = refs[2 * count :]
    step = pl.program_id(0)
    plane = lax.axis_index("seq") // per_plane
    me = lax.axis_index("mp")

    @pl.when(step == 0)
    def _():
        for place in range(count):
            gap = target(place, me, count) - plane
            for index, w_ref in enumerate(w_refs):

                @pl.when(gap == index - (count - 1))
                def _(w_ref=w_ref, place=place):
                    pltpu.make_async_copy(w_ref, held.at[place], sems.at[place]).start()

    pltpu.make_async_copy(w_refs[0], held.at[step], sems.at[step]).wait()
    product = dot(dq_ref[...], held[step], NT).astype(jnp.bfloat16)

    @pl.when(step < count // 2)
    def _():
        send_ref[0] = product

    @pl.when(step >= count // 2)
    def _():
        keep_ref[0] = product


def parts_call(count, per_plane, dq, blocks):
    rows, width = dq.shape
    depth = blocks[0].shape[0]
    half = count // 2
    shape = jax.ShapeDtypeStruct((half, rows, depth), jnp.bfloat16)
    return pl.pallas_call(
        functools.partial(parts_kernel, count, per_plane),
        grid=(count,),
        in_specs=[pl.BlockSpec((rows, width), lambda j: (0, 0))]
        + [pl.BlockSpec(memory_space=pl.ANY)] * len(blocks),
        out_specs=[
            pl.BlockSpec((1, rows, depth), lambda j: (jnp.minimum(j, half - 1), 0, 0)),
            pl.BlockSpec((1, rows, depth), lambda j: (jnp.maximum(j - half, 0), 0, 0)),
        ],
        out_shape=[shape, shape],
        scratch_shapes=[
            pltpu.VMEM((count, depth, width), jnp.bfloat16),
            pltpu.SemaphoreType.DMA((count,)),
        ],
        compiler_params=pltpu.CompilerParams(vmem_limit_bytes=32 << 20),
        cost_estimate=pl.CostEstimate(
            flops=rows * width * depth,
            bytes_accessed=2 * rows * width,
            transcendentals=0,
        ),
        name="parts",
    )(dq, *blocks)


def plane_routes(planes, per_plane, hop):
    seq_count = planes * per_plane
    up = [
        (s, s + per_plane) for s in range(seq_count - per_plane) if s // per_plane >= hop - 1
    ]
    return up, [(seq_count - 1 - a, seq_count - 1 - b) for a, b in up]


def plane_step(up, down, planes, per_plane, hop):
    up_route, down_route = plane_routes(planes, per_plane, hop)
    return lax.ppermute(up, "seq", up_route), lax.ppermute(down, "seq", down_route)


def shifted(block, distance, count):
    route = [(i - distance, i) for i in range(count) if 0 <= i - distance < count]
    return lax.ppermute(block, "seq", route)


def turned(block, distance, count, per_plane):
    route = [
        (s, s - s % per_plane + (s % per_plane + distance) % per_plane) for s in range(count)
    ]
    return lax.ppermute(block, "seq", route)


def summed(send, keep, count):
    if count != 4:
        parts = jnp.concatenate([send, keep], axis=0)
        return lax.psum_scatter(parts, "mp", scatter_dimension=0, tiled=True)[0]
    arrived = lax.ppermute(send, "mp", [(m, m ^ 1) for m in range(count)])
    wide = arrived.astype(jnp.float32) + keep.astype(jnp.float32)
    across = lax.ppermute(wide[0].astype(jnp.bfloat16), "mp", [(m, m ^ 2) for m in range(count)])
    return (wide[1] + across.astype(jnp.float32)).astype(jnp.bfloat16)


def local(
    win_query,
    win_key,
    win_value,
    win_dout,
    cross_query,
    cross_dout,
    patch_key,
    patch_value,
    patch_len,
    patch_owner,
    w_query,
):
    seq_count, mp_count = lax.axis_size("seq"), lax.axis_size("mp")
    per_plane = seq_count // mp_count
    planes = mp_count
    column = lax.axis_index("seq") % per_plane
    width = win_query.shape[1]
    patch_rows = patch_key.shape[0]

    low_rim = jnp.stack([win_key[:WIN], win_value[:WIN]])
    high_rim = jnp.stack([win_key[WIN:], win_value[WIN:]])
    patch_len, low_rim, high_rim = lax.optimization_barrier((patch_len, low_rim, high_rim))
    before = shifted(low_rim, 1, seq_count)
    after = shifted(high_rim, -1, seq_count)
    up, down = {0: w_query}, {0: w_query}
    up[1], down[1] = plane_step(w_query, w_query, planes, per_plane, 1)
    cap = max(2, 2 * (patch_rows // seq_count))
    cross_dq, slots = cross_call(
        cap, seq_count * cap, cross_query, cross_dout, patch_key, patch_value, patch_len, patch_owner
    )
    all_dq = [cross_dq] + [
        turned(cross_dq, r, seq_count, per_plane) for r in range(1, per_plane)
    ]
    up[1], down[1], slots, before, after = lax.optimization_barrier(
        (up[1], down[1], slots, before, after)
    )
    up[2], down[2] = plane_step(up[1], down[1], planes, per_plane, 2)
    win_dq, own_dk, own_dv, low_send, high_send = window_call(
        seq_count, win_query, win_key, win_value, win_dout, before, after
    )
    low_back = shifted(low_send, -1, seq_count)
    high_back = shifted(high_send, 1, seq_count)
    up[2], down[2], win_dq, *all_dq = lax.optimization_barrier(
        (up[2], down[2], win_dq, *all_dq)
    )
    for hop in range(3, planes):
        up[hop], down[hop] = plane_step(up[hop - 1], down[hop - 1], planes, per_plane, hop)
    last = planes - 1
    blocks = [up[hop] for hop in range(last, 0, -1)] + [down[hop] for hop in range(planes)]

    near = [None] * per_plane
    for r in range(per_plane - 1, -1, -1):
        if r == 0:
            all_dq[0], low_back, high_back = lax.optimization_barrier(
                (all_dq[0], low_back, high_back)
            )
        send, keep = parts_call(planes, per_plane, all_dq[r], blocks)
        if r == per_plane - 1:
            slots, send = lax.optimization_barrier((slots, send))
            arrived = lax.all_to_all(
                slots.reshape(2, seq_count, cap, width), "seq", split_axis=1, concat_axis=1, tiled=True
            )
        total = summed(send, keep, mp_count)
        near[r] = turned(total, -r, seq_count, per_plane) if r else total
    win_dk, win_dv = join_call(own_dk, own_dv, low_back, high_back)
    pieces = []
    for j in range(per_plane):
        piece = near[j]
        for x in range(1, per_plane):
            piece = jnp.where(column == x, near[(j - x) % per_plane], piece)
        pieces.append(piece)
    byte_grads = jnp.concatenate(pieces, axis=1)
    patch_grads = arrived.reshape(2, seq_count * cap, width)
    return (win_dq, win_dk, win_dv, patch_grads, byte_grads)


def solution(mesh):
    in_specs = (P("seq", "mp"),) * 8 + (P("seq", None),) * 2 + (P("seq", "mp"),)
    out_specs = (P("seq", "mp"),) * 3 + (P(None, "seq", "mp"), P("seq", "mp"))
    return jax.shard_map(local, mesh=mesh, in_specs=in_specs, out_specs=out_specs, check_vma=False)
```
